256 devices in a mesh: dp: 4 (over z_hi), gx: 16 (over z_lo, x, core), gy: 4 (over y).
Axes of the slice: x: 4, y: 4, z: 8 (z_hi: 4, z_lo: 2; z = z_hi * 2 + z_lo), core: 2. Of those that a mesh axis runs over, the one named last changes fastest.
Arguments:
- volume: bfloat16 [4, 64, 64, 8, 128], P('dp', 'gx', 'gy'), may hold values from -6 to 6
- cotangent: bfloat16 [4, 64, 64, 8, 128], P('dp', 'gx', 'gy'), may hold values from -0.3125 to 0.3125
- master: float32 [6912, 128], P('dp'), may hold values from -0.109375 to 0.109375
- moment_one: float32 [6912, 128], P('dp'), may hold values from -6 to 6
- moment_two: float32 [6912, 128], P('dp'), may hold values from 0.25 to 4
Outputs:
- activation: bfloat16 [4, 64, 64, 8, 128], P('dp', 'gx', 'gy')
- new_master: float32 [6912, 128], P('dp')
- new_moment_one: float32 [6912, 128], P('dp')
- new_moment_two: float32 [6912, 128], P('dp')
The draws below stay inside these ranges and needn't reach their ends.
All inputs are finite; a program needn't handle non-finite values.
Results may differ from the reference program's by a relative error of at most 0.006.
The reference program's roundings to bfloat16 on the way (of `kernels`, `hidden`, `delta_two` and `delta_one`) count: a program that leaves them out, or rounds other values in their place, can miss the bound.
Values may be sent and summed in bfloat16 or wider, within the bound.
No kernel may reach another device: no remote copies, remote signals or barrier semaphores. Data moves between devices by JAX's collectives and lax.ppermute only.
A program may use at most 64 MiB of HBM per device.

```python
import math
import jax
import jax.numpy as jnp
from jax import lax

C = 128
CZ = 8
VOLUMES = 4
NX = 64
NY = 64
PROWS = 6912


def shard_levels(stream_key, extent, cuts, low, high):
    gain, own = 1.0, jax.random.fold_in(stream_key, 6)
    for position, parts in cuts:
        draws = jnp.exp(jax.random.uniform(jax.random.fold_in(own, position), (parts,), jnp.float32, low / len(cuts), high / len(cuts)))
        gain = gain * jnp.repeat(draws, extent[position] // parts).reshape([-1 if axis == position else 1 for axis in range(len(extent))])
    return gain


def normal_values(key, shape, deviation, reach, split=(), held_as=jnp.bfloat16):
    loudness = shard_levels(key, shape, split, -0.22, 0.18) if split else 1.0
    entries = jax.random.normal(key, shape, jnp.float32) * deviation * loudness
    return jnp.minimum(jnp.maximum(entries, -reach), reach).astype(held_as)


def setup_inputs(seed: int = 0) -> dict:
    splits = jax.random.split(jax.random.key(seed), 6)
    volume = normal_values(splits[0], (VOLUMES, NX, NY, CZ, C), 1.0, 6.0, ((0, 4), (1, 16), (2, 4)))
    cotangent = normal_values(splits[1], (VOLUMES, NX, NY, CZ, C), (8.0 / (VOLUMES * NX * NY * CZ) ** 0.5), 0.3125, ((0, 4), (1, 16), (2, 4)))
    master = normal_values(splits[2], (PROWS, C), (27 * C) ** -0.5, 0.109375, ((0, 4),), jnp.float32)
    moment_one = normal_values(splits[3], (PROWS, C), 1.0, 6.0, ((0, 4),), jnp.float32)
    moment_two = jnp.clip(jnp.exp(math.log(4.0) - 2.7725887 * jax.random.uniform(splits[4], (PROWS, C), jnp.float32) ** shard_levels(splits[4], (PROWS, C), ((0, 4),), -0.2, 0.2)), 0.25, 4.0)
    return dict(volume=volume, cotangent=cotangent, master=master, moment_one=moment_one, moment_two=moment_two)


inv_root_two = 0.7071067811865476
inv_root_tau = 0.3989422804014327
beta_one = 0.9
beta_two = 0.999
learn_rate = 0.01
epsilon = 1e-08

def gelu_value(field):
    return 0.5 * field * (1.0 + lax.erf(field * inv_root_two))

def gelu_slope(field):
    normal_cdf = 0.5 * (1.0 + lax.erf(field * inv_root_two))
    return normal_cdf + field * jnp.exp(-0.5 * field * field) * inv_root_tau

def pad_all(field):
    return jnp.pad(field, ((1, 1), (1, 1), (1, 1), (0, 0)))

def convolve(padded, kernel):
    span_x = padded.shape[0] - 2
    span_y = padded.shape[1] - 2
    span_z = padded.shape[2] - 2
    total = jnp.zeros((span_x * span_y * span_z, kernel.shape[2]), jnp.float32)
    for offset_x in range(3):
        for offset_y in range(3):
            for offset_z in range(3):
                window = padded[offset_x:offset_x + span_x, offset_y:offset_y + span_y, offset_z:offset_z + span_z]
                total = total + jnp.dot(window.reshape(-1, padded.shape[3]), kernel[9 * offset_x + 3 * offset_y + offset_z], preferred_element_type=jnp.float32)
    return total.reshape(span_x, span_y, span_z, kernel.shape[2])

def kernel_grad(padded, delta):
    flat_delta = delta.reshape(-1, delta.shape[3])
    span_x, span_y, span_z = (delta.shape[0], delta.shape[1], delta.shape[2])
    pieces = []
    for offset_x in range(3):
        for offset_y in range(3):
            for offset_z in range(3):
                window = padded[offset_x:offset_x + span_x, offset_y:offset_y + span_y, offset_z:offset_z + span_z]
                pieces.append(jnp.dot(window.reshape(-1, padded.shape[3]).T, flat_delta, preferred_element_type=jnp.float32))
    return jnp.stack(pieces)

def adam_update(master, moment_one, moment_two, gradient):
    new_one = beta_one * moment_one + (1.0 - beta_one) * gradient
    new_two = beta_two * moment_two + (1.0 - beta_two) * gradient * gradient
    update = new_one / (1.0 - beta_one ** 10) / (jnp.sqrt(new_two / (1.0 - beta_two ** 10)) + epsilon)
    return (master - learn_rate * update, new_one, new_two)

def reference(volume, cotangent, master, moment_one, moment_two):
    kernels = master.astype(jnp.bfloat16).reshape(2, 27, C, C)
    flipped = kernels[1][::-1].transpose(0, 2, 1)

    def single(pair):
        field, upstream = pair
        padded_in = pad_all(field)
        first = convolve(padded_in, kernels[0])
        hidden = gelu_value(first).astype(jnp.bfloat16)
        padded_hidden = pad_all(hidden)
        second = convolve(padded_hidden, kernels[1])
        result = gelu_value(second).astype(jnp.bfloat16)
        delta_two = (upstream.astype(jnp.float32) * gelu_slope(second)).astype(jnp.bfloat16)
        grad_two = kernel_grad(padded_hidden, delta_two)
        back = convolve(pad_all(delta_two), flipped)
        delta_one = (back * gelu_slope(first)).astype(jnp.bfloat16)
        grad_one = kernel_grad(padded_in, delta_one)
        return (result, jnp.stack([grad_one, grad_two]))
    results, grads = lax.map(single, (volume, cotangent))
    gradient = lax.optimization_barrier(jnp.sum(grads, axis=0)).reshape(54 * C, C)
    new_master, new_one, new_two = adam_update(master, moment_one, moment_two, gradient)
    return (results, new_master, new_one, new_two)
```

```python
import jax
import jax.numpy as jnp
from jax import lax
from jax.experimental import pallas as pl
from jax.experimental.pallas import tpu as pltpu
from jax.sharding import Mesh
from jax.sharding import PartitionSpec as P

inv_root_two = 0.7071067811865476
inv_root_tau = 0.3989422804014327
beta_one = 0.9
beta_two = 0.999
learn_rate = 0.01
epsilon = 1e-08

BF = jnp.bfloat16
F32 = jnp.float32

C = 128
SX, SY, SZ = 4, 16, 8
NX, NY = 64, 64
TAPS = 14
HALF = TAPS // 2 * C
PIECE = HALF // 16


def gelu_value(field):
    return 0.5 * field * (1.0 + lax.erf(field * inv_root_two))


def gelu_slope(field):
    normal_cdf = 0.5 * (1.0 + lax.erf(field * inv_root_two))
    return normal_cdf + field * jnp.exp(-0.5 * field * field) * inv_root_tau


def depth_triple(field):
    depth = lax.broadcasted_iota(jnp.int32, field.shape, 2)
    below = jnp.where(depth == 0, 0.0, pltpu.roll(field, 1, 2))
    above = jnp.where(depth == SZ - 1, 0.0, pltpu.roll(field, SZ - 1, 2))
    return [part.reshape(-1, C).astype(BF) for part in (below, field, above)]


def store_triple(ref, rows, field):
    for position, part in enumerate(depth_triple(field)):
        ref[rows, position * C : (position + 1) * C] = part


def conv_rows(ref, planes_out, wide, weights):
    rows = planes_out * wide * SZ
    step = wide * SZ
    left = jnp.concatenate([ref[a * step : a * step + rows, :] for a in range(3)], axis=1)
    prod = jnp.dot(left, weights, preferred_element_type=F32).reshape(planes_out, wide, SZ, 3 * C)
    return (
        prod[:, 0 : wide - 2, :, 0:C]
        + prod[:, 1 : wide - 1, :, C : 2 * C]
        + prod[:, 2:wide, :, 2 * C : 3 * C]
    )


def layer_weights(taps, layer):
    columns = []
    for b in range(3):
        rows = [(layer * 27 + 9 * a + 3 * b) * C for a in range(3)]
        columns.append(jnp.concatenate([taps[r : r + 3 * C] for r in rows], axis=0))
    return jnp.concatenate(columns, axis=1)


def grad_taps(grads, layer, ref, wide, first_plane, shift, delta):
    lefts = []
    for b in range(3):
        before, after = shift + b, wide - SY - shift - b
        padded = jnp.concatenate(
            [
                jnp.zeros((SX, before, SZ, C), F32),
                delta,
                jnp.zeros((SX, after, SZ, C), F32),
            ],
            axis=1,
        ).reshape(SX * wide * SZ, C)
        lefts.append(jnp.transpose(padded).astype(BF))
    left = jnp.concatenate(lefts, axis=0)
    step = wide * SZ
    for a in range(3):
        start = (first_plane + a) * step
        prod = jnp.dot(left, ref[start : start + SX * step, :], preferred_element_type=F32)
        for b in range(3):
            for c in range(3):
                grads[layer * 27 + 9 * a + 3 * b + c] = prod[b * C : (b + 1) * C, c * C : (c + 1) * C]


def step_kernel(
    place, vol, left, right, low, high, cot, *rest
):
    pieces = rest[:8]
    act, send, keep = rest[8:11]
    taps, flipped, field, hid, dlt, grads = rest[11:]
    gx, gy, core = place[0], place[1], place[2]

    for index, piece in enumerate(pieces):
        owner_core = core if index < 4 else 1 - core
        owner_y = lax.rem(gy + 4 - index % 4, 4)
        taps[
            pl.ds(owner_core * 54, 54), pl.ds(pl.multiple_of(owner_y * 16, 16), 16), :
        ] = piece[...].reshape(54, 16, C)
    tap_rows = taps[...].reshape(54 * C, C)

    middle = [left[0:3], vol[...], right[0:3]]
    for part, planes, start in zip(middle, (3, 4, 3), (0, 3, 7)):
        whole = jnp.concatenate(
            [
                low[3 * start : 3 * (start + planes)].reshape(planes, 3, SZ, C),
                part,
                high[3 * start : 3 * (start + planes)].reshape(planes, 3, SZ, C),
            ],
            axis=1,
        ).astype(F32)
        store_triple(field, slice(start * 176, (start + planes) * 176), whole)

    first = conv_rows(field, 8, 22, layer_weights(tap_rows, 0))
    x_at = lax.broadcasted_iota(jnp.int32, first.shape, 0) + (gx * SX - 2)
    y_at = lax.broadcasted_iota(jnp.int32, first.shape, 1) + (gy * SY - 2)
    inside = (x_at >= 0) & (x_at < NX) & (y_at >= 0) & (y_at < NY)
    hidden = jnp.where(inside, gelu_value(first), 0.0)
    slope_one = gelu_slope(first[2:6, 2:18])
    store_triple(hid, slice(0, 8 * 160), hidden)

    second = conv_rows(hid, 6, 20, layer_weights(tap_rows, 1))
    act[...] = gelu_value(second[1:5, 1:17]).astype(BF)
    upstream = jnp.concatenate(
        [
            low[30:36].reshape(6, 1, SZ, C),
            jnp.concatenate([left[3:4], cot[...], right[3:4]], axis=0),
            high[30:36].reshape(6, 1, SZ, C),
        ],
        axis=1,
    ).astype(F32)
    delta_two = upstream * gelu_slope(second)
    store_triple(dlt, slice(0, 6 * 144), delta_two)
    grad_taps(grads, 1, hid, 20, 1, 1, delta_two[1:5, 1:17])

    for t in range(27):
        a, b, c = t // 9, t // 3 % 3, t % 3
        row = (27 + 26 - t) * C
        block = jnp.transpose(tap_rows[row : row + C].astype(F32)).astype(BF)
        flipped[(3 * a + c) * C : (3 * a + c + 1) * C, b * C : (b + 1) * C] = block
    back = conv_rows(dlt, 4, 18, flipped[...])
    grad_taps(grads, 0, field, 22, 2, 2, back * slope_one)

    for shard in range(4):
        base = 27 * (shard // 2) + 13 * (shard % 2)
        keep[shard] = grads[pl.ds(base + 7 * core, 7)].reshape(HALF, C)
        send[shard] = grads[pl.ds(base + 7 * (1 - core), 7)].reshape(HALF, C).astype(BF)


def device_step(place, vol, left, right, low, high, cot, pieces):
    vmem = pl.BlockSpec(memory_space=pltpu.VMEM)
    return pl.pallas_call(
        step_kernel,
        out_shape=(
            jax.ShapeDtypeStruct((SX, SY, SZ, C), BF),
            jax.ShapeDtypeStruct((4, HALF, C), BF),
            jax.ShapeDtypeStruct((4, HALF, C), F32),
        ),
        in_specs=[pl.BlockSpec(memory_space=pltpu.SMEM)] + [vmem] * 14,
        out_specs=(vmem, vmem, vmem),
        scratch_shapes=[
            pltpu.VMEM((108, 64, C), BF),
            pltpu.VMEM((9 * C, 3 * C), BF),
            pltpu.VMEM((10 * 176, 3 * C), BF),
            pltpu.VMEM((8 * 160, 3 * C), BF),
            pltpu.VMEM((6 * 144, 3 * C), BF),
            pltpu.VMEM((54, C, C), F32),
        ],
        compiler_params=pltpu.CompilerParams(vmem_limit_bytes=48 * 2**20),
        cost_estimate=pl.CostEstimate(flops=3_500_000_000, bytes_accessed=8_000_000, transcendentals=1_000_000),
        name="unet_step",
    )(place, vol, left, right, low, high, cot, *pieces)


def adam_kernel(place, mine, other, master, one, two, new_master, new_one, new_two, grad):
    core, odd = place[2], lax.rem(place[3], 2)
    for source, owner in ((mine, core), (other, 1 - core)):
        for tap in range(TAPS // 2):
            block = source[tap * C : (tap + 1) * C].astype(F32)
            grad[pl.ds(pl.multiple_of((owner * (TAPS // 2) + tap) * C, C), C), :] = jnp.transpose(block)
    rows = master.shape[0]
    gradient = grad[pl.ds(pl.multiple_of(odd * (C // 2), C // 2), rows), :]
    first = beta_one * one[...] + (1.0 - beta_one) * gradient
    second = beta_two * two[...] + (1.0 - beta_two) * gradient * gradient
    update = first / (1.0 - beta_one**10) / (jnp.sqrt(second / (1.0 - beta_two**10)) + epsilon)
    new_master[...] = master[...] - learn_rate * update
    new_one[...] = first
    new_two[...] = second


def adam_update(place, mine, other, master, one, two):
    vmem = pl.BlockSpec(memory_space=pltpu.VMEM)
    shape = jax.ShapeDtypeStruct(master.shape, F32)
    return pl.pallas_call(
        adam_kernel,
        out_shape=(shape, shape, shape),
        in_specs=[pl.BlockSpec(memory_space=pltpu.SMEM)] + [vmem] * 5,
        out_specs=(vmem, vmem, vmem),
        scratch_shapes=[pltpu.VMEM((TAPS * C, C), F32)],
        compiler_params=pltpu.CompilerParams(vmem_limit_bytes=24 * 2**20),
        name="adam_step",
    )(place, mine, other, master, one, two)


GX = ("zl", "x", "c")


def shifted(cells, axis, count, by):
    return lax.ppermute(cells, axis, [(i, (i + by) % count) for i in range(count)])


def gathered_weights(master, dp, core, gy):
    local = master.astype(BF).reshape(27, 64, C)
    own = lax.dynamic_slice(local, (0, 16 * gy, 0), (27, 16, C))
    got = [
        lax.ppermute(
            own,
            ("dp", "c"),
            [((d ^ s) * 2 + c, d * 2 + c) for d in range(4) for c in range(2) if (d ^ s) // 2 == c],
        )
        for s in (1, 2, 3)
    ]
    both = []
    for parity in range(2):
        distance = jnp.bitwise_xor(dp, 2 * core + parity)
        both.append(
            jnp.where(
                distance == 0,
                own,
                jnp.where(distance == 1, got[0], jnp.where(distance == 2, got[1], got[2])),
            )
        )
    stack = jnp.stack(both)
    mine = [stack] + [shifted(stack, "gy", 4, s) for s in (1, 2, 3)]
    return mine + [shifted(part, "c", 2, 1) for part in mine]


def per_device(volume, cotangent, master, moment_one, moment_two):
    vol, cot = volume[0], cotangent[0]
    dp, core, gy = lax.axis_index("dp"), lax.axis_index("c"), lax.axis_index("gy")
    gx = lax.axis_index(GX)
    place = jnp.stack([gx, gy, core, dp]).astype(jnp.int32)

    up_x = [(i, i + 1) for i in range(15)]
    down_x = [(i + 1, i) for i in range(15)]
    left = lax.ppermute(jnp.concatenate([vol[1:4], cot[3:4]]), GX, up_x)
    right = lax.ppermute(jnp.concatenate([vol[0:3], cot[0:1]]), GX, down_x)

    def edge(at, width, field):
        return field[:, at : at + width].reshape(-1, SZ, C)

    def side(at_field, at_cot):
        return jnp.concatenate(
            [
                edge(at_field, 3, left[0:3]),
                edge(at_field, 3, vol),
                edge(at_field, 3, right[0:3]),
                edge(at_cot, 1, left[3:4]),
                edge(at_cot, 1, cot),
                edge(at_cot, 1, right[3:4]),
            ]
        )

    low = lax.ppermute(side(SY - 3, SY - 1), "gy", [(i, i + 1) for i in range(3)])
    high = lax.ppermute(side(0, 0), "gy", [(i + 1, i) for i in range(3)])

    pieces = gathered_weights(master, dp, core, gy)
    act, send, keep = device_step(place, vol, left, right, low, high, cot, pieces)

    pair = (keep + shifted(send, "c", 2, 1).astype(F32)).astype(BF)
    spread = pair.reshape(4, 16, PIECE, C).transpose(1, 0, 2, 3)
    plane = lax.all_to_all(spread, ("x", "gy"), 0, 0)
    plane = jnp.sum(plane.astype(F32), axis=0).astype(BF)
    twice = jnp.broadcast_to(plane[:, None], (4, 2, PIECE, C)).reshape(8, PIECE, C)
    column = lax.all_to_all(twice, ("dp", "zl"), 0, 0)
    column = jnp.sum(column.astype(F32), axis=0).astype(BF)
    mine = lax.all_to_all(jnp.broadcast_to(column, (16, PIECE, C)), ("x", "gy"), 0, 0).reshape(HALF, C)
    other = shifted(mine, "c", 2, 1)
    new_master, new_one, new_two = adam_update(place, mine, other, master, moment_one, moment_two)
    return (act[None], new_master, new_one, new_two)


def solution(mesh):
    fine = Mesh(mesh.devices.reshape(4, 2, 4, 2, 4), ("dp", "zl", "x", "c", "gy"))
    cells = P("dp", GX, "gy", None, None)
    rows = P("dp", None)
    return jax.shard_map(
        per_device,
        mesh=fine,
        in_specs=(cells, cells, rows, rows, rows),
        out_specs=(cells, rows, rows, rows),
        check_vma=False,
    )
```

```python
import jax
import jax.numpy as jnp
from jax import lax
from jax.experimental import pallas as pl
from jax.experimental.pallas import tpu as pltpu
from jax.sharding import Mesh
from jax.sharding import PartitionSpec as P

inv_root_two = 0.7071067811865476
inv_root_tau = 0.3989422804014327
beta_one = 0.9
beta_two = 0.999
learn_rate = 0.01
epsilon = 1e-08

BF = jnp.bfloat16
F32 = jnp.float32

C = 128
SX, SY, SZ = 4, 16, 8
NX, NY = 64, 64
TAPS = 14
HALF = TAPS // 2 * C
PIECE = HALF // 16


def position():
    x, core, gy = lax.axis_index("x"), lax.axis_index("c"), lax.axis_index("gy")
    gx = (lax.axis_index("zl") * 4 + x) * 2 + core
    return gx, gy, core, lax.axis_index("dp"), gy ^ (2 * lax.rem(x, 2) + lax.div(x, 2))


def gelu_value(field):
    return 0.5 * field * (1.0 + lax.erf(field * inv_root_two))


def gelu_slope(field):
    normal_cdf = 0.5 * (1.0 + lax.erf(field * inv_root_two))
    return normal_cdf + field * jnp.exp(-0.5 * field * field) * inv_root_tau


def depth_triple(field):
    depth = lax.broadcasted_iota(jnp.int32, field.shape, 2)
    below = jnp.where(depth == 0, 0.0, pltpu.roll(field, 1, 2))
    above = jnp.where(depth == SZ - 1, 0.0, pltpu.roll(field, SZ - 1, 2))
    return [part.reshape(-1, C).astype(BF) for part in (below, field, above)]


def store_triple(ref, rows, field):
    for position, part in enumerate(depth_triple(field)):
        ref[rows, position * C : (position + 1) * C] = part


def conv_rows(ref, planes_out, wide, weights):
    rows = planes_out * wide * SZ
    step = wide * SZ
    left = jnp.concatenate([ref[a * step : a * step + rows, :] for a in range(3)], axis=1)
    prod = jnp.dot(left, weights, preferred_element_type=F32).reshape(planes_out, wide, SZ, 3 * C)
    return (
        prod[:, 0 : wide - 2, :, 0:C]
        + prod[:, 1 : wide - 1, :, C : 2 * C]
        + prod[:, 2:wide, :, 2 * C : 3 * C]
    )


def layer_weights(taps, layer):
    columns = []
    for b in range(3):
        rows = [(layer * 27 + 9 * a + 3 * b) * C for a in range(3)]
        columns.append(jnp.concatenate([taps[r : r + 3 * C] for r in rows], axis=0))
    return jnp.concatenate(columns, axis=1)


def grad_taps(grads, layer, ref, wide, first_plane, shift, delta):
    lefts = []
    for b in range(3):
        before, after = shift + b, wide - SY - shift - b
        padded = jnp.concatenate(
            [
                jnp.zeros((SX, before, SZ, C), F32),
                delta,
                jnp.zeros((SX, after, SZ, C), F32),
            ],
            axis=1,
        ).reshape(SX * wide * SZ, C)
        lefts.append(jnp.transpose(padded).astype(BF))
    left = jnp.concatenate(lefts, axis=0)
    step = wide * SZ
    for a in range(3):
        start = (first_plane + a) * step
        prod = jnp.dot(left, ref[start : start + SX * step, :], preferred_element_type=F32)
        for b in range(3):
            for c in range(3):
                grads[layer * 27 + 9 * a + 3 * b + c] = prod[b * C : (b + 1) * C, c * C : (c + 1) * C]


def payload_kernel(vol, cot, master, whole, half, near, far, first, last, rows, sems):
    gx, gy, core, dp, quarter = position()
    moves = [
        (master.at[:, pl.ds(pl.multiple_of(16 * quarter, 16), 16), :], rows),
        (vol.at[pl.ds(1 - core, 3)], near.at[0:3]),
        (vol.at[pl.ds(core, 3)], far.at[0:3]),
        (cot.at[pl.ds(3 * (1 - core), 1)], near.at[3:4]),
        (cot.at[pl.ds(3 * core, 1)], far.at[3:4]),
        (vol.at[:, 0:3], first.at[:, 0:3]),
        (cot.at[:, 0:1], first.at[:, 3:4]),
        (vol.at[:, SY - 3 : SY], last.at[:, 0:3]),
        (cot.at[:, SY - 1 : SY], last.at[:, 3:4]),
    ]
    copies = [pltpu.make_async_copy(src, dst, sems.at[i]) for i, (src, dst) in enumerate(moves)]
    for copy in copies:
        copy.start()
    copies[0].wait()
    whole[...] = rows[...].astype(BF)
    half[...] = rows[pl.ds(13 * core, 14)].astype(BF)
    for copy in copies[1:]:
        copy.wait()


def payloads(vol, cot, master):
    vmem = pl.BlockSpec(memory_space=pltpu.VMEM)
    hbm = pl.BlockSpec(memory_space=pltpu.HBM)
    side = pltpu.VMEM((4, SY, SZ, C), BF)
    edge = pltpu.VMEM((4, 4, SZ, C), BF)
    return pl.pallas_call(
        payload_kernel,
        out_shape=(
            pltpu.VMEM((27, 16, C), BF),
            pltpu.VMEM((14, 16, C), BF),
            side,
            side,
            edge,
            edge,
        ),
        in_specs=[hbm] * 3,
        out_specs=(vmem,) * 6,
        scratch_shapes=[pltpu.VMEM((27, 16, C), F32), pltpu.SemaphoreType.DMA((9,))],
        compiler_params=pltpu.CompilerParams(vmem_limit_bytes=8 * 2**20),
        name="payloads",
    )(*(pltpu.with_memory_space_constraint(a, pltpu.HBM) for a in (vol, cot, master.reshape(27, 64, C))))


SIDE = 36 * SZ // 16


def relay_kernel(stack, near, far, first, last, even, odd):
    gx, gy, core, dp, quarter = position()
    parity = lax.rem(gy, 2)
    even[0:41] = stack[...]
    odd[0:41] = stack[...]
    for out, upper in ((even, 1 - parity), (odd, parity)):
        own = jnp.where(upper == 0, first[...].astype(F32), last[...].astype(F32)).astype(BF)
        groups = []
        for part, planes in ((near, 3), (own, 4), (far, 3)):
            rows = part[:, 0:3] if planes == 4 else part[0:3, pl.ds(upper * (SY - 3), 3)]
            groups.append(rows.reshape(-1, SZ, C))
        for part, planes in ((near, 1), (own, 4), (far, 1)):
            rows = part[:, 3:4] if planes == 4 else part[3:4, pl.ds(upper * (SY - 1), 1)]
            groups.append(rows.reshape(-1, SZ, C))
        out[41 : 41 + SIDE] = jnp.concatenate(groups).reshape(SIDE, 16, C)


def relay(stack, near, far, first, last):
    vmem = pl.BlockSpec(memory_space=pltpu.VMEM)
    both = jax.ShapeDtypeStruct((41 + SIDE, 16, C), BF)
    return pl.pallas_call(
        relay_kernel,
        out_shape=(both, both),
        in_specs=[vmem] * 5,
        out_specs=(vmem,) * 2,
        compiler_params=pltpu.CompilerParams(vmem_limit_bytes=8 * 2**20),
        name="relay",
    )(stack, near, far, first, last)


def prepare_kernel(vol, cot, near, far, even, odd, field, upstream):
    gx, gy, core, dp, quarter = position()
    parity = lax.rem(gy, 2)

    def ordered(first, second, swap):
        return jnp.where(swap == 0, first, second), jnp.where(swap == 0, second, first)

    left, right = ordered(far[...].astype(F32), near[...].astype(F32), core)
    even_side = even[41 : 41 + SIDE].reshape(36, SZ, C).astype(F32)
    odd_side = odd[41 : 41 + SIDE].reshape(36, SZ, C).astype(F32)
    low, high = ordered(odd_side, even_side, parity)
    low = jnp.where(gy == 0, 0.0, low)
    high = jnp.where(gy == 3, 0.0, high)
    sides = []
    for side in (low, high):
        lower, upper = ordered(side[21:30], side[0:9], core)
        sides.append(jnp.concatenate([lower, side[9:21], upper]).reshape(10, 3, SZ, C))
        lower, upper = ordered(side[35:36], side[30:31], core)
        sides.append(jnp.concatenate([lower, side[31:35], upper]).reshape(6, 1, SZ, C))
    own = jnp.concatenate([left[0:3], vol[...].astype(F32), right[0:3]], axis=0)
    store_triple(field, slice(0, 1760), jnp.concatenate([sides[0], own, sides[2]], axis=1))
    own = jnp.concatenate([left[3:4], cot[...].astype(F32), right[3:4]], axis=0)
    upstream[...] = jnp.concatenate([sides[1], own, sides[3]], axis=1)


def prepare(vol, cot, near, far, even, odd):
    vmem = pl.BlockSpec(memory_space=pltpu.VMEM)
    return pl.pallas_call(
        prepare_kernel,
        out_shape=(
            jax.ShapeDtypeStruct((10 * 176, 3 * C), BF),
            jax.ShapeDtypeStruct((6, 18, SZ, C), F32),
        ),
        in_specs=[vmem] * 6,
        out_specs=(vmem, vmem),
        compiler_params=pltpu.CompilerParams(vmem_limit_bytes=16 * 2**20),
        cost_estimate=pl.CostEstimate(flops=4_000_000, bytes_accessed=3_000_000, transcendentals=0),
        name="prepare",
    )(vol, cot, near, far, even, odd)


def step_kernel(field, upstream, master, *rest):
    pieces = rest[:8]
    act, send, keep = rest[8:11]
    taps, flipped, hid, dlt, grads = rest[11:]
    gx, gy, core, dp, quarter = position()

    taps[pl.ds(dp * 27, 27)] = master[...].astype(BF).reshape(27, 64, C)
    for index, piece in enumerate(pieces):
        owner_core = core if index < 4 else 1 - core
        rows = pl.ds(pl.multiple_of((quarter ^ (0, 1, 3, 2)[index % 4]) * 16, 16), 16)
        whole = dp ^ (1 + owner_core)
        taps[pl.ds(whole * 27, 27), rows, :] = piece[0:27]
        taps[pl.ds((dp ^ 3) * 27 + 13 * owner_core, 14), rows, :] = piece[27:41]
    tap_rows = taps[...].reshape(54 * C, C)

    first = conv_rows(field, 8, 22, layer_weights(tap_rows, 0))
    x_at = lax.broadcasted_iota(jnp.int32, first.shape, 0) + (gx * SX - 2)
    y_at = lax.broadcasted_iota(jnp.int32, first.shape, 1) + (gy * SY - 2)
    inside = (x_at >= 0) & (x_at < NX) & (y_at >= 0) & (y_at < NY)
    hidden = jnp.where(inside, gelu_value(first), 0.0)
    slope_one = gelu_slope(first[2:6, 2:18])
    store_triple(hid, slice(0, 8 * 160), hidden)

    second = conv_rows(hid, 6, 20, layer_weights(tap_rows, 1))
    act[...] = gelu_value(second[1:5, 1:17]).astype(BF)
    delta_two = upstream[...] * gelu_slope(second)
    store_triple(dlt, slice(0, 6 * 144), delta_two)
    grad_taps(grads, 1, hid, 20, 1, 1, delta_two[1:5, 1:17])

    for t in range(27):
        a, b, c = t // 9, t // 3 % 3, t % 3
        row = (27 + 26 - t) * C
        block = jnp.transpose(tap_rows[row : row + C].astype(F32)).astype(BF)
        flipped[(3 * a + c) * C : (3 * a + c + 1) * C, b * C : (b + 1) * C] = block
    back = conv_rows(dlt, 4, 18, flipped[...])
    grad_taps(grads, 0, field, 22, 2, 2, back * slope_one)

    for shard in range(4):
        base = 27 * (shard // 2) + 13 * (shard % 2)
        keep[shard] = grads[pl.ds(base + 7 * core, 7)].reshape(HALF, C)
        send[shard] = grads[pl.ds(base + 7 * (1 - core), 7)].reshape(HALF, C).astype(BF)


def device_step(field, upstream, master, pieces):
    vmem = pl.BlockSpec(memory_space=pltpu.VMEM)
    return pl.pallas_call(
        step_kernel,
        out_shape=(
            jax.ShapeDtypeStruct((SX, SY, SZ, C), BF),
            jax.ShapeDtypeStruct((4, HALF, C), BF),
            jax.ShapeDtypeStruct((4, HALF, C), F32),
        ),
        in_specs=[vmem] * 11,
        out_specs=(vmem, vmem, vmem),
        scratch_shapes=[
            pltpu.VMEM((108, 64, C), BF),
            pltpu.VMEM((9 * C, 3 * C), BF),
            pltpu.VMEM((8 * 160, 3 * C), BF),
            pltpu.VMEM((6 * 144, 3 * C), BF),
            pltpu.VMEM((54, C, C), F32),
        ],
        compiler_params=pltpu.CompilerParams(vmem_limit_bytes=44 * 2**20),
        cost_estimate=pl.CostEstimate(flops=3_500_000_000, bytes_accessed=8_000_000, transcendentals=1_000_000),
        name="unet_step",
    )(field, upstream, master, *pieces)


ADAM_ROWS = 576


def adam_kernel(mine, other, master, one, two, new_master, new_one, new_two, grad, parts, sems):
    gx, gy, core, dp, quarter = position()
    odd = lax.rem(dp, 2)
    for source, owner in ((mine, core), (other, 1 - core)):
        for tap in range(TAPS // 2):
            block = source[tap * C : (tap + 1) * C].astype(F32)
            grad[pl.ds(pl.multiple_of((owner * (TAPS // 2) + tap) * C, C), C), :] = jnp.transpose(block)
    copies = []
    for chunk in range(master.shape[0] // ADAM_ROWS):
        rows = pl.ds(chunk * ADAM_ROWS, ADAM_ROWS)
        shifted_rows = pl.ds(pl.multiple_of(odd * (C // 2) + chunk * ADAM_ROWS, C // 2), ADAM_ROWS)
        gradient = grad[shifted_rows, :]
        first = beta_one * one[rows, :] + (1.0 - beta_one) * gradient
        second = beta_two * two[rows, :] + (1.0 - beta_two) * gradient * gradient
        update = first / (1.0 - beta_one**10) / (jnp.sqrt(second / (1.0 - beta_two**10)) + epsilon)
        parts[0, rows, :] = master[rows, :] - learn_rate * update
        parts[1, rows, :] = first
        parts[2, rows, :] = second
        for index, out in enumerate((new_master, new_one, new_two)):
            copy = pltpu.make_async_copy(parts.at[index, rows], out.at[rows], sems.at[chunk, index])
            copy.start()
            copies.append(copy)
    for copy in copies:
        copy.wait()


def adam_update(mine, other, master, one, two):
    vmem = pl.BlockSpec(memory_space=pltpu.VMEM)
    hbm = pl.BlockSpec(memory_space=pl.ANY)
    shape = jax.ShapeDtypeStruct(master.shape, F32)
    return pl.pallas_call(
        adam_kernel,
        out_shape=(shape, shape, shape),
        in_specs=[vmem] * 5,
        out_specs=(hbm, hbm, hbm),
        scratch_shapes=[
            pltpu.VMEM((TAPS * C, C), F32),
            pltpu.VMEM((3,) + master.shape, F32),
            pltpu.SemaphoreType.DMA((master.shape[0] // ADAM_ROWS, 3)),
        ],
        compiler_params=pltpu.CompilerParams(vmem_limit_bytes=24 * 2**20),
        name="adam_step",
    )(mine, other, master, one, two)


GX = ("zl", "x", "c")


def exchanged(cells, axis, count, by):
    return lax.ppermute(cells, axis, [(i, i ^ by) for i in range(count)])


def paired(cells, axis, count):
    pairs = [(i, i + 1) for i in range(1, count - 1, 2)]
    return lax.ppermute(cells, axis, pairs + [(j, i) for i, j in pairs])


def over_dp(whole, half):
    whole = lax.ppermute(
        whole, ("dp", "c"), [(2 * d + c, 2 * (d ^ (1 + c)) + c) for d in range(4) for c in range(2)]
    )
    return whole, exchanged(half, "dp", 4, 3)


def per_device(volume, cotangent, master, moment_one, moment_two):
    vol, cot = volume[0], cotangent[0]
    whole, half, near, far, first, last = payloads(vol, cot, master)
    whole, half = over_dp(whole, half)
    near = exchanged(near, "c", 2, 1)
    far = paired(far, GX, 16)

    stack = jnp.concatenate([whole, half])
    opposite = exchanged(stack, "x", 4, 1)
    even, odd = relay(stack, near, far, first, last)
    odd = exchanged(odd, "gy", 4, 3)
    even = exchanged(even, "gy", 4, 1)
    mine = [stack, even, odd, opposite]
    pieces = mine + [exchanged(part, "c", 2, 1) for part in mine]
    field, upstream = prepare(vol, cot, near, far, even, odd)
    act, send, keep = device_step(field, upstream, master, pieces)

    pair = (keep + exchanged(send, "c", 2, 1).astype(F32)).astype(BF)
    spread = pair.reshape(4, 16, PIECE, C).transpose(1, 0, 2, 3).reshape(16, 4 * PIECE, C)
    plane = lax.all_to_all(spread, ("x", "gy"), 0, 0)
    plane = jnp.sum(plane.astype(F32), axis=0).astype(BF).reshape(4, PIECE, C)
    twice = jnp.broadcast_to(plane[:, None], (4, 2, PIECE, C)).reshape(8, PIECE, C)
    column = lax.all_to_all(twice, ("dp", "zl"), 0, 0)
    column = jnp.sum(column.astype(F32), axis=0).astype(BF)
    mine = lax.all_to_all(jnp.broadcast_to(column, (16, PIECE, C)), ("x", "gy"), 0, 0).reshape(HALF, C)
    other = exchanged(mine, "c", 2, 1)
    new_master, new_one, new_two = adam_update(mine, other, master, moment_one, moment_two)
    return (act[None], new_master, new_one, new_two)


def solution(mesh):
    fine = Mesh(mesh.devices.reshape(4, 2, 4, 2, 4), ("dp", "zl", "x", "c", "gy"))
    cells = P("dp", GX, "gy", None, None)
    rows = P("dp", None)
    return jax.shard_map(
        per_device,
        mesh=fine,
        in_specs=(cells, cells, rows, rows, rows),
        out_specs=(cells, rows, rows, rows),
        check_vma=False,
    )
```

```python
import functools

import jax
import jax.numpy as jnp
from jax import lax
from jax.experimental import pallas as pl
from jax.experimental.pallas import tpu as pltpu
from jax.sharding import Mesh
from jax.sharding import PartitionSpec as P

inv_root_two = 0.7071067811865476
inv_root_tau = 0.3989422804014327
beta_one = 0.9
beta_two = 0.999
learn_rate = 0.01
epsilon = 1e-08

BF = jnp.bfloat16
F32 = jnp.float32

C = 128
SX, SY, SZ = 4, 16, 8
NX, NY = 64, 64
TAPS = 14
HALF = TAPS // 2 * C
PIECE = HALF // 16


def position():
    x, core, gy = lax.axis_index("x"), lax.axis_index("c"), lax.axis_index("gy")
    gx = (lax.axis_index("zl") * 4 + x) * 2 + core
    return gx, gy, core, lax.axis_index("dp"), gy ^ (2 * lax.rem(x, 2) + lax.div(x, 2))


def gelu_value(field):
    return 0.5 * field * (1.0 + lax.erf(field * inv_root_two))


def gelu_slope(field):
    normal_cdf = 0.5 * (1.0 + lax.erf(field * inv_root_two))
    return normal_cdf + field * jnp.exp(-0.5 * field * field) * inv_root_tau


def depth_triple(field):
    depth = lax.broadcasted_iota(jnp.int32, field.shape, 2)
    below = jnp.where(depth == 0, 0.0, pltpu.roll(field, 1, 2))
    above = jnp.where(depth == SZ - 1, 0.0, pltpu.roll(field, SZ - 1, 2))
    return [part.reshape(-1, C).astype(BF) for part in (below, field, above)]


def store_triple(ref, rows, field):
    for position, part in enumerate(depth_triple(field)):
        ref[rows, position * C : (position + 1) * C] = part


def conv_rows(ref, planes_out, wide, weights):
    rows = planes_out * wide * SZ
    step = wide * SZ
    left = jnp.concatenate([ref[a * step : a * step + rows, :] for a in range(3)], axis=1)
    prod = jnp.dot(left, weights, preferred_element_type=F32).reshape(planes_out, wide, SZ, 3 * C)
    return (
        prod[:, 0 : wide - 2, :, 0:C]
        + prod[:, 1 : wide - 1, :, C : 2 * C]
        + prod[:, 2:wide, :, 2 * C : 3 * C]
    )


def layer_weights(taps, layer):
    columns = []
    for b in range(3):
        rows = [(layer * 27 + 9 * a + 3 * b) * C for a in range(3)]
        columns.append(jnp.concatenate([taps[r : r + 3 * C] for r in rows], axis=0))
    return jnp.concatenate(columns, axis=1)


def grad_taps(grads, layer, ref, wide, first_plane, shift, delta):
    lefts = []
    for b in range(3):
        before, after = shift + b, wide - SY - shift - b
        padded = jnp.concatenate(
            [
                jnp.zeros((SX, before, SZ, C), F32),
                delta,
                jnp.zeros((SX, after, SZ, C), F32),
            ],
            axis=1,
        ).reshape(SX * wide * SZ, C)
        lefts.append(jnp.transpose(padded).astype(BF))
    left = jnp.concatenate(lefts, axis=0)
    step = wide * SZ
    starts = [(first_plane + a) * step for a in range(3)]
    right = jnp.concatenate([ref[start : start + SX * step, :] for start in starts], axis=1)
    prod = jnp.dot(left, right, preferred_element_type=F32)
    for tap in range(27):
        a, b, c = tap // 9, tap // 3 % 3, tap % 3
        column = (3 * a + c) * C
        grads[layer * 27 + tap] = prod[b * C : (b + 1) * C, column : column + C]


def payload_kernel(vol, cot, master, whole, half, near, far, vol_out, cot_out, rows, sems):
    gx, gy, core, dp, quarter = position()
    moves = [
        (master.at[:, pl.ds(pl.multiple_of(16 * quarter, 16), 16), :], rows),
        (vol.at[pl.ds(core, 3)], far.at[0:3]),
        (cot.at[pl.ds(3 * core, 1)], far.at[3:4]),
        (vol.at[pl.ds(1 - core, 3)], near.at[0:3]),
        (cot.at[pl.ds(3 * (1 - core), 1)], near.at[3:4]),
        (vol, vol_out),
        (cot, cot_out),
    ]
    copies = [pltpu.make_async_copy(src, dst, sems.at[i]) for i, (src, dst) in enumerate(moves)]
    for copy in copies:
        copy.start()
    copies[0].wait()
    whole[...] = rows[...].astype(BF)
    half[...] = rows[pl.ds(13 * core, 14)].astype(BF)
    for copy in copies[1:]:
        copy.wait()


def payloads(vol, cot, master):
    vmem = pl.BlockSpec(memory_space=pltpu.VMEM)
    hbm = pl.BlockSpec(memory_space=pltpu.HBM)
    cells = pltpu.VMEM((4, SY, SZ, C), BF)
    return pl.pallas_call(
        payload_kernel,
        out_shape=(pltpu.VMEM((27, 16, C), BF), pltpu.VMEM((14, 16, C), BF)) + (cells,) * 4,
        in_specs=[hbm] * 3,
        out_specs=(vmem,) * 6,
        scratch_shapes=[pltpu.VMEM((27, 16, C), F32), pltpu.SemaphoreType.DMA((7,))],
        compiler_params=pltpu.CompilerParams(vmem_limit_bytes=8 * 2**20),
        name="payloads",
    )(*(pltpu.with_memory_space_constraint(a, pltpu.HBM) for a in (vol, cot, master.reshape(27, 64, C))))


SIDE = 26 * SZ // 16


def relay_kernel(stack, vol, cot, far, even, odd):
    gx, gy, core, dp, quarter = position()
    parity = lax.rem(gy, 2)
    for out, upper in ((even, 1 - parity), (odd, parity)):
        three, one = pl.ds(upper * (SY - 3), 3), pl.ds(upper * (SY - 1), 1)
        groups = [vol[:, three], far[0:3, three], cot[:, one], far[3:4, one]]
        out[0:41] = stack[...]
        out[41 : 41 + SIDE] = jnp.concatenate([g.reshape(-1, SZ, C) for g in groups]).reshape(SIDE, 16, C)


def relay(stack, vol, cot, far):
    vmem = pl.BlockSpec(memory_space=pltpu.VMEM)
    both = jax.ShapeDtypeStruct((41 + SIDE, 16, C), BF)
    return pl.pallas_call(
        relay_kernel,
        out_shape=(both, both),
        in_specs=[vmem] * 4,
        out_specs=(vmem,) * 2,
        compiler_params=pltpu.CompilerParams(vmem_limit_bytes=8 * 2**20),
        name="relay",
    )(stack, vol, cot, far)


def prepare_kernel(vol, cot, near, far, even, odd, mate_even, mate_odd, field, upstream):
    gx, gy, core, dp, quarter = position()
    parity = lax.rem(gy, 2)

    def ordered(first, second, swap):
        return jnp.where(swap == 0, first, second), jnp.where(swap == 0, second, first)

    def side_of(ref):
        return ref[41 : 41 + SIDE].reshape(26, SZ, C).astype(F32)

    left, right = ordered(far[...].astype(F32), near[...].astype(F32), core)
    sides = []
    lower, upper = ordered(side_of(odd), side_of(even), parity)
    mate_lower, mate_upper = ordered(side_of(mate_odd), side_of(mate_even), parity)
    for side, mate, outside in ((lower, mate_lower, gy == 0), (upper, mate_upper, gy == 3)):
        mate_planes = jnp.where(core == 0, mate[0:9], mate[3:12])
        mate_plane = jnp.where(core == 0, mate[21:22], mate[24:25])
        first, last = ordered(side[12:21], mate_planes, core)
        planes = jnp.concatenate([first, side[0:12], last]).reshape(10, 3, SZ, C)
        sides.append(jnp.where(outside, 0.0, planes))
        first, last = ordered(side[25:26], mate_plane, core)
        planes = jnp.concatenate([first, side[21:25], last]).reshape(6, 1, SZ, C)
        sides.append(jnp.where(outside, 0.0, planes))
    own = jnp.concatenate([left[0:3], vol[...].astype(F32), right[0:3]], axis=0)
    store_triple(field, slice(0, 1760), jnp.concatenate([sides[0], own, sides[2]], axis=1))
    own = jnp.concatenate([left[3:4], cot[...].astype(F32), right[3:4]], axis=0)
    upstream[...] = jnp.concatenate([sides[1], own, sides[3]], axis=1)


def prepare(vol, cot, near, far, even, odd, mate_even, mate_odd):
    vmem = pl.BlockSpec(memory_space=pltpu.VMEM)
    return pl.pallas_call(
        prepare_kernel,
        out_shape=(
            jax.ShapeDtypeStruct((10 * 176, 3 * C), BF),
            jax.ShapeDtypeStruct((6, 18, SZ, C), F32),
        ),
        in_specs=[vmem] * 8,
        out_specs=(vmem, vmem),
        compiler_params=pltpu.CompilerParams(vmem_limit_bytes=16 * 2**20),
        cost_estimate=pl.CostEstimate(flops=4_000_000, bytes_accessed=3_000_000, transcendentals=0),
        name="prepare",
    )(vol, cot, near, far, even, odd, mate_even, mate_odd)


def step_kernel(field, upstream, master, *rest):
    pieces = rest[:8]
    act, send, keep = rest[8:11]
    taps, flipped, hid, dlt, grads = rest[11:]
    gx, gy, core, dp, quarter = position()

    taps[pl.ds(dp * 27, 27)] = master[...].astype(BF).reshape(27, 64, C)
    for index, piece in enumerate(pieces):
        owner_core = core if index < 4 else 1 - core
        rows = pl.ds(pl.multiple_of((quarter ^ (0, 1, 3, 2)[index % 4]) * 16, 16), 16)
        whole = dp ^ (1 + 2 * owner_core)
        taps[pl.ds(whole * 27, 27), rows, :] = piece[0:27]
        taps[pl.ds((dp ^ 2) * 27 + 13 * owner_core, 14), rows, :] = piece[27:41]
    tap_rows = taps[...].reshape(54 * C, C)

    first = conv_rows(field, 8, 22, layer_weights(tap_rows, 0))
    x_at = lax.broadcasted_iota(jnp.int32, first.shape, 0) + (gx * SX - 2)
    y_at = lax.broadcasted_iota(jnp.int32, first.shape, 1) + (gy * SY - 2)
    inside = (x_at >= 0) & (x_at < NX) & (y_at >= 0) & (y_at < NY)
    hidden = jnp.where(inside, gelu_value(first), 0.0)
    slope_one = gelu_slope(first[2:6, 2:18])
    store_triple(hid, slice(0, 8 * 160), hidden)

    second = conv_rows(hid, 6, 20, layer_weights(tap_rows, 1))
    act[...] = gelu_value(second[1:5, 1:17]).astype(BF)
    delta_two = upstream[...] * gelu_slope(second)
    store_triple(dlt, slice(0, 6 * 144), delta_two)
    grad_taps(grads, 1, hid, 20, 1, 1, delta_two[1:5, 1:17])

    for t in range(27):
        a, b, c = t // 9, t // 3 % 3, t % 3
        row = (27 + 26 - t) * C
        block = jnp.transpose(tap_rows[row : row + C].astype(F32)).astype(BF)
        flipped[(3 * a + c) * C : (3 * a + c + 1) * C, b * C : (b + 1) * C] = block
    back = conv_rows(dlt, 4, 18, flipped[...])
    grad_taps(grads, 0, field, 22, 2, 2, back * slope_one)

    for shard in range(4):
        base = 27 * (shard // 2) + 13 * (shard % 2)
        keep[shard] = grads[pl.ds(base + 7 * core, 7)].reshape(HALF, C)
        send[shard] = grads[pl.ds(base + 7 * (1 - core), 7)].reshape(HALF, C).astype(BF)


def device_step(field, upstream, master, pieces):
    vmem = pl.BlockSpec(memory_space=pltpu.VMEM)
    return pl.pallas_call(
        step_kernel,
        out_shape=(
            jax.ShapeDtypeStruct((SX, SY, SZ, C), BF),
            jax.ShapeDtypeStruct((4, HALF, C), BF),
            jax.ShapeDtypeStruct((4, HALF, C), F32),
        ),
        in_specs=[vmem] * 11,
        out_specs=(vmem, vmem, vmem),
        scratch_shapes=[
            pltpu.VMEM((108, 64, C), BF),
            pltpu.VMEM((9 * C, 3 * C), BF),
            pltpu.VMEM((8 * 160, 3 * C), BF),
            pltpu.VMEM((6 * 144, 3 * C), BF),
            pltpu.VMEM((54, C, C), F32),
        ],
        compiler_params=pltpu.CompilerParams(vmem_limit_bytes=44 * 2**20),
        cost_estimate=pl.CostEstimate(flops=3_500_000_000, bytes_accessed=8_000_000, transcendentals=1_000_000),
        name="unet_step",
    )(field, upstream, master, *pieces)


def plane_kernel(parts, out):
    for shard in range(4):
        total = parts[0, shard].astype(F32)
        for sender in range(1, 16):
            total = total + parts[sender, shard].astype(F32)
        out[2 * shard] = total.astype(BF)
        out[2 * shard + 1] = total.astype(BF)


def plane_sum(parts):
    vmem = pl.BlockSpec(memory_space=pltpu.VMEM)
    return pl.pallas_call(
        plane_kernel,
        out_shape=jax.ShapeDtypeStruct((8, PIECE, C), BF),
        in_specs=[vmem],
        out_specs=vmem,
        compiler_params=pltpu.CompilerParams(vmem_limit_bytes=8 * 2**20),
        name="plane_sum",
    )(parts)


OWN_ROWS = HALF - C // 2
CHUNKS = 4


def adam_kernel(own_step, rows_now, *refs):
    sources, (master, one, two) = refs[: 1 if own_step else 2], refs[1 if own_step else 2 :][:3]
    new_master, new_one, new_two, grad, parts, sems = refs[-6:]
    core, odd = lax.axis_index("c"), lax.rem(lax.axis_index("dp"), 2)
    half = TAPS // 2
    owned = ((sources[0], core, range(half)),)
    if not own_step:
        owned = ((sources[1], 1 - core, range(half)), (sources[0], core, (half - 1, 0)))
    for source, owner, taps in owned:
        for tap in taps:
            block = jnp.transpose(source[tap * C : (tap + 1) * C].astype(F32))
            grad[pl.ds(pl.multiple_of((owner * half + tap) * C, C), C), :] = block
    begin = core * HALF if own_step else (1 - core) * OWN_ROWS
    size = rows_now // CHUNKS
    copies = []
    for chunk in range(CHUNKS):
        start = pl.multiple_of(begin + chunk * size, 16)
        rows, held = pl.ds(start, size), pl.ds(chunk * size, size)
        gradient = grad[pl.ds(pl.multiple_of(start + odd * (C // 2), 16), size), :]
        first = beta_one * one[rows, :] + (1.0 - beta_one) * gradient
        second = beta_two * two[rows, :] + (1.0 - beta_two) * gradient * gradient
        update = first / (1.0 - beta_one**10) / (jnp.sqrt(second / (1.0 - beta_two**10)) + epsilon)
        parts[0, held, :] = master[rows, :] - learn_rate * update
        parts[1, held, :] = first
        parts[2, held, :] = second
        for index, out in enumerate((new_master, new_one, new_two)):
            copy = pltpu.make_async_copy(parts.at[index, held], out.at[rows], sems.at[chunk, index])
            copy.start()
            copies.append(copy)
    for copy in copies:
        copy.wait()


def adam_step(own_step, sources, state, held=()):
    rows_now = OWN_ROWS if own_step else state[0].shape[0] - OWN_ROWS
    vmem = pl.BlockSpec(memory_space=pltpu.VMEM)
    hbm = pl.BlockSpec(memory_space=pl.ANY)
    inputs = len(sources) + len(state)
    return pl.pallas_call(
        functools.partial(adam_kernel, own_step, rows_now),
        out_shape=(jax.ShapeDtypeStruct(state[0].shape, F32),) * 3,
        in_specs=[vmem] * inputs + [hbm] * len(held),
        out_specs=(hbm,) * 3,
        input_output_aliases={inputs + i: i for i in range(len(held))},
        scratch_shapes=[
            pltpu.VMEM((TAPS * C, C), F32),
            pltpu.VMEM((3, rows_now, C), F32),
            pltpu.SemaphoreType.DMA((CHUNKS, 3)),
        ],
        compiler_params=pltpu.CompilerParams(vmem_limit_bytes=16 * 2**20),
        cost_estimate=pl.CostEstimate(flops=3_000_000, bytes_accessed=4_000_000, transcendentals=200_000),
        name="adam_own" if own_step else "adam_rest",
    )(*sources, *state, *held)


GX = ("zl", "x", "c")


def exchanged(cells, axis, count, by):
    return lax.ppermute(cells, axis, [(i, i ^ by) for i in range(count)])


def paired(cells, axis, count):
    pairs = [(i, i + 1) for i in range(1, count - 1, 2)]
    return lax.ppermute(cells, axis, pairs + [(j, i) for i, j in pairs])


def over_dp(whole, half):
    whole = lax.ppermute(
        whole, ("dp", "c"), [(2 * d + c, 2 * (d ^ (1 + 2 * c)) + c) for d in range(4) for c in range(2)]
    )
    return whole, exchanged(half, "dp", 4, 2)


def per_device(volume, cotangent, master, moment_one, moment_two):
    vol, cot = volume[0], cotangent[0]
    whole, half, near, far, vol, cot = payloads(vol, cot, master)
    whole, half = over_dp(whole, half)
    far = paired(far, GX, 16)
    near = exchanged(near, "c", 2, 1)

    stack = jnp.concatenate([whole, half])
    opposite = exchanged(stack, "x", 4, 1)
    even, odd = relay(stack, vol, cot, far)
    odd = exchanged(odd, "gy", 4, 3)
    even = exchanged(even, "gy", 4, 1)
    even, odd, near = lax.optimization_barrier((even, odd, near))
    mine = [stack, even, odd, opposite]
    mates = [exchanged(part, "c", 2, 1) for part in mine]
    pieces = mine + mates
    field, upstream = prepare(vol, cot, near, far, even, odd, mates[1], mates[2])
    act, send, keep = device_step(field, upstream, master, pieces)

    pair = (keep + exchanged(send, "c", 2, 1).astype(F32)).astype(BF)
    spread = pair.reshape(4, 16, PIECE, C).transpose(1, 0, 2, 3).reshape(16, 4 * PIECE, C)
    plane = lax.all_to_all(spread, ("x", "gy"), 0, 0)
    column = lax.all_to_all(plane_sum(plane.reshape(16, 4, PIECE, C)), ("dp", "zl"), 0, 0)
    column = jnp.sum(column.astype(F32), axis=0).astype(BF)
    mine = lax.all_to_all(jnp.broadcast_to(column, (16, PIECE, C)), ("x", "gy"), 0, 0).reshape(HALF, C)
    other = exchanged(mine, "c", 2, 1)
    state = (master, moment_one, moment_two)
    held = adam_step(True, (mine,), state)
    new_master, new_one, new_two = adam_step(False, (mine, other), state, held)
    return (act[None], new_master, new_one, new_two)


def solution(mesh):
    fine = Mesh(mesh.devices.reshape(4, 2, 4, 2, 4), ("dp", "zl", "x", "c", "gy"))
    cells = P("dp", GX, "gy", None, None)
    rows = P("dp", None)
    return jax.shard_map(
        per_device,
        mesh=fine,
        in_specs=(cells, cells, rows, rows, rows),
        out_specs=(cells, rows, rows, rows),
        check_vma=False,
    )
```

```python
import functools

import jax
import jax.numpy as jnp
from jax import lax
from jax.experimental import pallas as pl
from jax.experimental.pallas import tpu as pltpu
from jax.sharding import Mesh
from jax.sharding import PartitionSpec as P

inv_root_two = 0.7071067811865476
inv_root_tau = 0.3989422804014327
beta_one = 0.9
beta_two = 0.999
learn_rate = 0.01
epsilon = 1e-08

BF = jnp.bfloat16
F32 = jnp.float32

C = 128
SX, SY, SZ = 4, 16, 8
NX, NY = 64, 64
PLANES_ONE, PLANES_TWO, PLANES_BACK = 2, 3, 2
TAPS = 14
HALF = TAPS // 2 * C
PIECE = HALF // 16


def position():
    x, core, gy = lax.axis_index("x"), lax.axis_index("c"), lax.axis_index("gy")
    gx = (lax.axis_index("zl") * 4 + x) * 2 + core
    return gx, gy, core, lax.axis_index("dp"), gy ^ (2 * lax.rem(x, 2) + lax.div(x, 2))


def gelu_value(field):
    return 0.5 * field * (1.0 + lax.erf(field * inv_root_two))


def gelu_slope(field):
    normal_cdf = 0.5 * (1.0 + lax.erf(field * inv_root_two))
    return normal_cdf + field * jnp.exp(-0.5 * field * field) * inv_root_tau


def depth_triple(field):
    depth = lax.broadcasted_iota(jnp.int32, field.shape, 2)
    below = jnp.where(depth == 0, 0.0, pltpu.roll(field, 1, 2))
    above = jnp.where(depth == SZ - 1, 0.0, pltpu.roll(field, SZ - 1, 2))
    return [part.reshape(-1, C).astype(BF) for part in (below, field, above)]


def store_triple(ref, rows, field):
    for position, part in enumerate(depth_triple(field)):
        ref[rows, position * C : (position + 1) * C] = part


def conv_planes(ref, first, planes_out, wide, weights):
    rows = planes_out * wide * SZ
    step = wide * SZ
    starts = [(first + a) * step for a in range(3)]
    left = jnp.concatenate([ref[start : start + rows, :] for start in starts], axis=1)
    prod = jnp.dot(left, weights, preferred_element_type=F32).reshape(planes_out, wide, SZ, 3 * C)
    return (
        prod[:, 0 : wide - 2, :, 0:C]
        + prod[:, 1 : wide - 1, :, C : 2 * C]
        + prod[:, 2:wide, :, 2 * C : 3 * C]
    )


def layer_weights(taps, layer):
    columns = []
    for b in range(3):
        rows = [(layer * 27 + 9 * a + 3 * b) * C for a in range(3)]
        columns.append(jnp.concatenate([taps[r : r + 3 * C] for r in rows], axis=0))
    return jnp.concatenate(columns, axis=1)


def grad_taps(grads, ref, wide, first_plane, shift, delta):
    lefts = []
    for b in range(3):
        before, after = shift + b, wide - SY - shift - b
        padded = jnp.concatenate(
            [
                jnp.zeros((SX, before, SZ, C), F32),
                delta,
                jnp.zeros((SX, after, SZ, C), F32),
            ],
            axis=1,
        ).reshape(SX * wide * SZ, C)
        lefts.append(jnp.transpose(padded).astype(BF))
    left = jnp.concatenate(lefts, axis=0)
    step = wide * SZ
    starts = [(first_plane + a) * step for a in range(3)]
    right = jnp.concatenate([ref[start : start + SX * step, :] for start in starts], axis=1)
    prod = jnp.dot(left, right, preferred_element_type=F32)
    for tap in range(27):
        a, b, c = tap // 9, tap // 3 % 3, tap % 3
        column = (3 * a + c) * C
        grads[tap] = prod[b * C : (b + 1) * C, column : column + C]


def payload_kernel(vol, cot, master, whole, half, near, far, vol_out, cot_out, rows, sems):
    gx, gy, core, dp, quarter = position()
    moves = [
        (master.at[:, pl.ds(pl.multiple_of(16 * quarter, 16), 16), :], rows),
        (vol.at[pl.ds(core, 3)], far.at[0:3]),
        (cot.at[pl.ds(3 * core, 1)], far.at[3:4]),
        (vol.at[pl.ds(1 - core, 3)], near.at[0:3]),
        (cot.at[pl.ds(3 * (1 - core), 1)], near.at[3:4]),
        (vol, vol_out),
        (cot, cot_out),
    ]
    copies = [pltpu.make_async_copy(src, dst, sems.at[i]) for i, (src, dst) in enumerate(moves)]
    for copy in copies:
        copy.start()
    copies[0].wait()
    whole[...] = rows[...].astype(BF)
    half[...] = rows[pl.ds(13 * core, 14)].astype(BF)
    for copy in copies[1:]:
        copy.wait()


def payloads(vol, cot, master):
    vmem = pl.BlockSpec(memory_space=pltpu.VMEM)
    hbm = pl.BlockSpec(memory_space=pltpu.HBM)
    cells = pltpu.VMEM((4, SY, SZ, C), BF)
    return pl.pallas_call(
        payload_kernel,
        out_shape=(pltpu.VMEM((27, 16, C), BF), pltpu.VMEM((14, 16, C), BF)) + (cells,) * 4,
        in_specs=[hbm] * 3,
        out_specs=(vmem,) * 6,
        scratch_shapes=[pltpu.VMEM((27, 16, C), F32), pltpu.SemaphoreType.DMA((7,))],
        compiler_params=pltpu.CompilerParams(vmem_limit_bytes=8 * 2**20),
        name="payloads",
    )(*(pltpu.with_memory_space_constraint(a, pltpu.HBM) for a in (vol, cot, master.reshape(27, 64, C))))


SIDE = 26 * SZ // 16


def relay_kernel(stack, vol, cot, far, even, odd):
    gx, gy, core, dp, quarter = position()
    parity = lax.rem(gy, 2)
    for out, upper in ((even, 1 - parity), (odd, parity)):
        three, one = pl.ds(upper * (SY - 3), 3), pl.ds(upper * (SY - 1), 1)
        groups = [vol[:, three], far[0:3, three], cot[:, one], far[3:4, one]]
        out[0:41] = stack[...]
        out[41 : 41 + SIDE] = jnp.concatenate([g.reshape(-1, SZ, C) for g in groups]).reshape(SIDE, 16, C)


def relay(stack, vol, cot, far):
    vmem = pl.BlockSpec(memory_space=pltpu.VMEM)
    both = jax.ShapeDtypeStruct((41 + SIDE, 16, C), BF)
    return pl.pallas_call(
        relay_kernel,
        out_shape=(both, both),
        in_specs=[vmem] * 4,
        out_specs=(vmem,) * 2,
        compiler_params=pltpu.CompilerParams(vmem_limit_bytes=8 * 2**20),
        name="relay",
    )(stack, vol, cot, far)


def prepare_kernel(vol, cot, near, far, even, odd, mate_even, mate_odd, field, upstream):
    gx, gy, core, dp, quarter = position()
    parity = lax.rem(gy, 2)

    def ordered(first, second, swap):
        return jnp.where(swap == 0, first, second), jnp.where(swap == 0, second, first)

    def side_of(ref):
        return ref[41 : 41 + SIDE].reshape(26, SZ, C).astype(F32)

    left, right = ordered(far[...].astype(F32), near[...].astype(F32), core)
    sides = []
    lower, upper = ordered(side_of(odd), side_of(even), parity)
    mate_lower, mate_upper = ordered(side_of(mate_odd), side_of(mate_even), parity)
    for side, mate, outside in ((lower, mate_lower, gy == 0), (upper, mate_upper, gy == 3)):
        mate_planes = jnp.where(core == 0, mate[0:9], mate[3:12])
        mate_plane = jnp.where(core == 0, mate[21:22], mate[24:25])
        first, last = ordered(side[12:21], mate_planes, core)
        planes = jnp.concatenate([first, side[0:12], last]).reshape(10, 3, SZ, C)
        sides.append(jnp.where(outside, 0.0, planes))
        first, last = ordered(side[25:26], mate_plane, core)
        planes = jnp.concatenate([first, side[21:25], last]).reshape(6, 1, SZ, C)
        sides.append(jnp.where(outside, 0.0, planes))
    own = jnp.concatenate([left[0:3], vol[...].astype(F32), right[0:3]], axis=0)
    store_triple(field, slice(0, 1760), jnp.concatenate([sides[0], own, sides[2]], axis=1))
    own = jnp.concatenate([left[3:4], cot[...].astype(F32), right[3:4]], axis=0)
    upstream[...] = jnp.concatenate([sides[1], own, sides[3]], axis=1)


def prepare(vol, cot, near, far, even, odd, mate_even, mate_odd):
    vmem = pl.BlockSpec(memory_space=pltpu.VMEM)
    return pl.pallas_call(
        prepare_kernel,
        out_shape=(
            jax.ShapeDtypeStruct((10 * 176, 3 * C), BF),
            jax.ShapeDtypeStruct((6, 18, SZ, C), F32),
        ),
        in_specs=[vmem] * 8,
        out_specs=(vmem, vmem),
        compiler_params=pltpu.CompilerParams(vmem_limit_bytes=16 * 2**20),
        cost_estimate=pl.CostEstimate(flops=4_000_000, bytes_accessed=3_000_000, transcendentals=0),
        name="prepare",
    )(vol, cot, near, far, even, odd, mate_even, mate_odd)


def halves(grads, core, keep, send):
    for shard in range(2):
        keep[shard] = grads[pl.ds(13 * shard + 7 * core, 7)].reshape(16, PIECE, C)
        send[shard] = grads[pl.ds(13 * shard + 7 * (1 - core), 7)].reshape(16, PIECE, C).astype(send.dtype)


def forward_kernel(field, upstream, master, *rest):
    pieces = rest[:8]
    act, dlt, slope, flipped, send, keep = rest[8:14]
    taps, hid, grads = rest[14:]
    gx, gy, core, dp, quarter = position()

    taps[pl.ds(dp * 27, 27)] = master[...].astype(BF).reshape(27, 64, C)
    for index, piece in enumerate(pieces):
        owner_core = core if index < 4 else 1 - core
        rows = pl.ds(pl.multiple_of((quarter ^ (0, 1, 3, 2)[index % 4]) * 16, 16), 16)
        whole = dp ^ (1 + 2 * owner_core)
        taps[pl.ds(whole * 27, 27), rows, :] = piece[0:27]
        taps[pl.ds((dp ^ 2) * 27 + 13 * owner_core, 14), rows, :] = piece[27:41]
    tap_rows = taps[...].reshape(54 * C, C)

    weights = layer_weights(tap_rows, 0)
    slopes = []
    for at in range(0, 8, PLANES_ONE):
        first = conv_planes(field, at, PLANES_ONE, 22, weights)
        x_at = lax.broadcasted_iota(jnp.int32, first.shape, 0) + (gx * SX - 2 + at)
        y_at = lax.broadcasted_iota(jnp.int32, first.shape, 1) + (gy * SY - 2)
        inside = (x_at >= 0) & (x_at < NX) & (y_at >= 0) & (y_at < NY)
        store_triple(hid, slice(at * 160, (at + PLANES_ONE) * 160), jnp.where(inside, gelu_value(first), 0.0))
        begin, end = max(at, 2) - at, min(at + PLANES_ONE, 6) - at
        if begin < end:
            slopes.append(gelu_slope(first[begin:end, 2:18]))
    slope[...] = jnp.concatenate(slopes)

    weights = layer_weights(tap_rows, 1)
    deltas = []
    for at in range(0, 6, PLANES_TWO):
        second = conv_planes(hid, at, PLANES_TWO, 20, weights)
        delta = upstream[at : at + PLANES_TWO] * gelu_slope(second)
        store_triple(dlt, slice(at * 144, (at + PLANES_TWO) * 144), delta)
        begin, end = max(at, 1) - at, min(at + PLANES_TWO, 5) - at
        if begin < end:
            act[at + begin - 1 : at + end - 1] = gelu_value(second[begin:end, 1:17]).astype(BF)
            deltas.append(delta[begin:end, 1:17])
    grad_taps(grads, hid, 20, 1, 1, jnp.concatenate(deltas))
    halves(grads, core, keep, send)

    for t in range(27):
        a, b, c = t // 9, t // 3 % 3, t % 3
        row = (27 + 26 - t) * C
        block = jnp.transpose(tap_rows[row : row + C].astype(F32)).astype(BF)
        flipped[(3 * a + c) * C : (3 * a + c + 1) * C, b * C : (b + 1) * C] = block


def backward_kernel(field, dlt, slope, flipped, send, keep, grads):
    weights = flipped[...]
    back = [conv_planes(dlt, at, PLANES_BACK, 18, weights) for at in range(0, 4, PLANES_BACK)]
    grad_taps(grads, field, 22, 2, 2, jnp.concatenate(back) * slope[...])
    halves(grads, lax.axis_index("c"), keep, send)


GRADIENT = (2, 16, PIECE, C)


def forward(field, upstream, master, pieces):
    vmem = pl.BlockSpec(memory_space=pltpu.VMEM)
    return pl.pallas_call(
        forward_kernel,
        out_shape=(
            jax.ShapeDtypeStruct((SX, SY, SZ, C), BF),
            jax.ShapeDtypeStruct((6 * 144, 3 * C), BF),
            jax.ShapeDtypeStruct((SX, SY, SZ, C), F32),
            jax.ShapeDtypeStruct((9 * C, 3 * C), BF),
            jax.ShapeDtypeStruct(GRADIENT, F32),
            jax.ShapeDtypeStruct(GRADIENT, F32),
        ),
        in_specs=[vmem] * 11,
        out_specs=(vmem,) * 6,
        scratch_shapes=[
            pltpu.VMEM((108, 64, C), BF),
            pltpu.VMEM((8 * 160, 3 * C), BF),
            pltpu.VMEM((27, C, C), F32),
        ],
        compiler_params=pltpu.CompilerParams(vmem_limit_bytes=40 * 2**20),
        cost_estimate=pl.CostEstimate(flops=2_500_000_000, bytes_accessed=8_000_000, transcendentals=1_000_000),
        name="forward",
    )(field, upstream, master, *pieces)


def backward(field, dlt, slope, flipped):
    vmem = pl.BlockSpec(memory_space=pltpu.VMEM)
    return pl.pallas_call(
        backward_kernel,
        out_shape=(jax.ShapeDtypeStruct(GRADIENT, BF), jax.ShapeDtypeStruct(GRADIENT, F32)),
        in_specs=[vmem] * 4,
        out_specs=(vmem,) * 2,
        scratch_shapes=[pltpu.VMEM((27, C, C), F32)],
        compiler_params=pltpu.CompilerParams(vmem_limit_bytes=32 * 2**20),
        cost_estimate=pl.CostEstimate(flops=8_000_000_000, bytes_accessed=8_000_000, transcendentals=0),
        name="backward",
    )(field, dlt, slope, flipped)


def pair_kernel(keep_one, got_one, keep_two, got_two, out):
    for layer, (keep, got) in enumerate(((keep_one, got_one), (keep_two, got_two))):
        for shard in range(2):
            total = keep[shard] + got[shard].astype(F32)
            for piece in range(16):
                out[piece, 2 * layer + shard] = total[piece].astype(BF)


def pair_sum(keep_one, got_one, keep_two, got_two):
    vmem = pl.BlockSpec(memory_space=pltpu.VMEM)
    return pl.pallas_call(
        pair_kernel,
        out_shape=jax.ShapeDtypeStruct((16, 4, PIECE, C), BF),
        in_specs=[vmem] * 4,
        out_specs=vmem,
        compiler_params=pltpu.CompilerParams(vmem_limit_bytes=16 * 2**20),
        name="pair_sum",
    )(keep_one, got_one, keep_two, got_two)


def plane_kernel(parts, out):
    for shard in range(4):
        total = parts[0, shard].astype(F32)
        for sender in range(1, 16):
            total = total + parts[sender, shard].astype(F32)
        out[2 * shard] = total.astype(BF)
        out[2 * shard + 1] = total.astype(BF)


def plane_sum(parts):
    vmem = pl.BlockSpec(memory_space=pltpu.VMEM)
    return pl.pallas_call(
        plane_kernel,
        out_shape=jax.ShapeDtypeStruct((8, PIECE, C), BF),
        in_specs=[vmem],
        out_specs=vmem,
        compiler_params=pltpu.CompilerParams(vmem_limit_bytes=8 * 2**20),
        name="plane_sum",
    )(parts)


OWN_ROWS = HALF - C // 2
CHUNKS = 4


def adam_kernel(own_step, rows_now, *refs):
    sources, (master, one, two) = refs[: 1 if own_step else 2], refs[1 if own_step else 2 :][:3]
    new_master, new_one, new_two, grad, parts, sems = refs[-6:]
    core, odd = lax.axis_index("c"), lax.rem(lax.axis_index("dp"), 2)
    half = TAPS // 2
    owned = ((sources[0], core, range(half)),)
    if not own_step:
        owned = ((sources[1], 1 - core, range(half)), (sources[0], core, (half - 1, 0)))
    for source, owner, taps in owned:
        for tap in taps:
            block = jnp.transpose(source[tap * C : (tap + 1) * C].astype(F32))
            grad[pl.ds(pl.multiple_of((owner * half + tap) * C, C), C), :] = block
    begin = core * HALF if own_step else (1 - core) * OWN_ROWS
    size = rows_now // CHUNKS
    copies = []
    for chunk in range(CHUNKS):
        start = pl.multiple_of(begin + chunk * size, 16)
        rows, held = pl.ds(start, size), pl.ds(chunk * size, size)
        gradient = grad[pl.ds(pl.multiple_of(start + odd * (C // 2), 16), size), :]
        first = beta_one * one[rows, :] + (1.0 - beta_one) * gradient
        second = beta_two * two[rows, :] + (1.0 - beta_two) * gradient * gradient
        update = first / (1.0 - beta_one**10) / (jnp.sqrt(second / (1.0 - beta_two**10)) + epsilon)
        parts[0, held, :] = master[rows, :] - learn_rate * update
        parts[1, held, :] = first
        parts[2, held, :] = second
        for index, out in enumerate((new_master, new_one, new_two)):
            copy = pltpu.make_async_copy(parts.at[index, held], out.at[rows], sems.at[chunk, index])
            copy.start()
            copies.append(copy)
    for copy in copies:
        copy.wait()


def adam_step(own_step, sources, state, held=()):
    rows_now = OWN_ROWS if own_step else state[0].shape[0] - OWN_ROWS
    vmem = pl.BlockSpec(memory_space=pltpu.VMEM)
    hbm = pl.BlockSpec(memory_space=pl.ANY)
    inputs = len(sources) + len(state)
    return pl.pallas_call(
        functools.partial(adam_kernel, own_step, rows_now),
        out_shape=(jax.ShapeDtypeStruct(state[0].shape, F32),) * 3,
        in_specs=[vmem] * inputs + [hbm] * len(held),
        out_specs=(hbm,) * 3,
        input_output_aliases={inputs + i: i for i in range(len(held))},
        scratch_shapes=[
            pltpu.VMEM((TAPS * C, C), F32),
            pltpu.VMEM((3, rows_now, C), F32),
            pltpu.SemaphoreType.DMA((CHUNKS, 3)),
        ],
        compiler_params=pltpu.CompilerParams(vmem_limit_bytes=16 * 2**20),
        cost_estimate=pl.CostEstimate(flops=3_000_000, bytes_accessed=4_000_000, transcendentals=200_000),
        name="adam_own" if own_step else "adam_rest",
    )(*sources, *state, *held)


GX = ("zl", "x", "c")


def exchanged(cells, axis, count, by):
    return lax.ppermute(cells, axis, [(i, i ^ by) for i in range(count)])


def paired(cells, axis, count):
    pairs = [(i, i + 1) for i in range(1, count - 1, 2)]
    return lax.ppermute(cells, axis, pairs + [(j, i) for i, j in pairs])


def over_dp(whole, half):
    whole = lax.ppermute(
        whole, ("dp", "c"), [(2 * d + c, 2 * (d ^ (1 + 2 * c)) + c) for d in range(4) for c in range(2)]
    )
    return whole, exchanged(half, "dp", 4, 2)


def per_device(volume, cotangent, master, moment_one, moment_two):
    vol, cot = volume[0], cotangent[0]
    whole, half, near, far, vol, cot = payloads(vol, cot, master)
    whole, half = over_dp(whole, half)
    far = paired(far, GX, 16)
    near = exchanged(near, "c", 2, 1)

    stack = jnp.concatenate([whole, half])
    opposite = exchanged(stack, "x", 4, 1)
    even, odd = relay(stack, vol, cot, far)
    odd = exchanged(odd, "gy", 4, 3)
    even = exchanged(even, "gy", 4, 1)
    even, odd, near = lax.optimization_barrier((even, odd, near))
    mine = [stack, even, odd, opposite]
    mates = [exchanged(part, "c", 2, 1) for part in mine]
    pieces = mine + mates
    field, upstream = prepare(vol, cot, near, far, even, odd, mates[1], mates[2])
    act, dlt, slope, flipped, send_two, keep_two = forward(field, upstream, master, pieces)
    got_two = exchanged(send_two, "c", 2, 1)
    send_one, keep_one = backward(field, dlt, slope, flipped)
    got_one = exchanged(send_one, "c", 2, 1)

    spread = pair_sum(keep_one, got_one, keep_two, got_two).reshape(16, 4 * PIECE, C)
    plane = lax.all_to_all(spread, ("x", "gy"), 0, 0)
    column = lax.all_to_all(plane_sum(plane.reshape(16, 4, PIECE, C)), ("dp", "zl"), 0, 0)
    column = jnp.sum(column.astype(F32), axis=0).astype(BF)
    mine = lax.all_to_all(jnp.broadcast_to(column, (16, PIECE, C)), ("x", "gy"), 0, 0).reshape(HALF, C)
    other = exchanged(mine, "c", 2, 1)
    state = (master, moment_one, moment_two)
    held = adam_step(True, (mine,), state)
    new_master, new_one, new_two = adam_step(False, (mine, other), state, held)
    return (act[None], new_master, new_one, new_two)


def solution(mesh):
    fine = Mesh(mesh.devices.reshape(4, 2, 4, 2, 4), ("dp", "zl", "x", "c", "gy"))
    cells = P("dp", GX, "gy", None, None)
    rows = P("dp", None)
    return jax.shard_map(
        per_device,
        mesh=fine,
        in_specs=(cells, cells, rows, rows, rows),
        out_specs=(cells, rows, rows, rows),
        check_vma=False,
    )
```

```python
import functools

import jax
import jax.numpy as jnp
from jax import lax
from jax.experimental import pallas as pl
from jax.experimental.pallas import tpu as pltpu
from jax.sharding import Mesh
from jax.sharding import PartitionSpec as P

inv_root_two = 0.7071067811865476
inv_root_tau = 0.3989422804014327
beta_one = 0.9
beta_two = 0.999
learn_rate = 0.01
epsilon = 1e-08

BF = jnp.bfloat16
F32 = jnp.float32

C = 128
SX, SY, SZ = 4, 16, 8
NX, NY = 64, 64
PLANES_ONE, PLANES_TWO, PLANES_BACK = 2, 3, 2
TAPS = 14
HALF = TAPS // 2 * C
PIECE = HALF // 16


def position():
    x, core, gy = lax.axis_index("x"), lax.axis_index("c"), lax.axis_index("gy")
    gx = (lax.axis_index("zl") * 4 + x) * 2 + core
    return gx, gy, core, lax.axis_index("dp"), gy ^ (2 * lax.rem(x, 2) + lax.div(x, 2))


def gelu_value(field):
    return 0.5 * field * (1.0 + lax.erf(field * inv_root_two))


def gelu_slope(field):
    normal_cdf = 0.5 * (1.0 + lax.erf(field * inv_root_two))
    return normal_cdf + field * jnp.exp(-0.5 * field * field) * inv_root_tau


def depth_triple(field):
    depth = lax.broadcasted_iota(jnp.int32, field.shape, 2)
    below = jnp.where(depth == 0, 0.0, pltpu.roll(field, 1, 2))
    above = jnp.where(depth == SZ - 1, 0.0, pltpu.roll(field, SZ - 1, 2))
    return [part.reshape(-1, C).astype(BF) for part in (below, field, above)]


def store_triple(ref, rows, field):
    for position, part in enumerate(depth_triple(field)):
        ref[rows, position * C : (position + 1) * C] = part


def conv_planes(ref, first, planes_out, wide, weights):
    rows = planes_out * wide * SZ
    step = wide * SZ
    starts = [(first + a) * step for a in range(3)]
    left = jnp.concatenate([ref[start : start + rows, :] for start in starts], axis=1)
    prod = jnp.dot(left, weights, preferred_element_type=F32).reshape(planes_out, wide, SZ, 3 * C)
    return (
        prod[:, 0 : wide - 2, :, 0:C]
        + prod[:, 1 : wide - 1, :, C : 2 * C]
        + prod[:, 2:wide, :, 2 * C : 3 * C]
    )


def layer_weights(taps, layer):
    columns = []
    for b in range(3):
        rows = [(layer * 27 + 9 * a + 3 * b) * C for a in range(3)]
        columns.append(jnp.concatenate([taps[r : r + 3 * C] for r in rows], axis=0))
    return jnp.concatenate(columns, axis=1)


def grad_taps(grads, ref, wide, first_plane, shift, delta):
    lefts = []
    for b in range(3):
        before, after = shift + b, wide - SY - shift - b
        padded = jnp.concatenate(
            [
                jnp.zeros((SX, before, SZ, C), F32),
                delta,
                jnp.zeros((SX, after, SZ, C), F32),
            ],
            axis=1,
        ).reshape(SX * wide * SZ, C)
        lefts.append(jnp.transpose(padded).astype(BF))
    left = jnp.concatenate(lefts, axis=0)
    step = wide * SZ
    starts = [(first_plane + a) * step for a in range(3)]
    right = jnp.concatenate([ref[start : start + SX * step, :] for start in starts], axis=1)
    prod = jnp.dot(left, right, preferred_element_type=F32)
    for tap in range(27):
        a, b, c = tap // 9, tap // 3 % 3, tap % 3
        column = (3 * a + c) * C
        grads[tap] = prod[b * C : (b + 1) * C, column : column + C]


def payload_kernel(vol, cot, master, whole, half, near, far, vol_out, cot_out, rows, sems):
    gx, gy, core, dp, quarter = position()
    moves = [
        (master.at[:, pl.ds(pl.multiple_of(16 * quarter, 16), 16), :], rows),
        (vol.at[pl.ds(core, 3)], far.at[0:3]),
        (cot.at[pl.ds(3 * core, 1)], far.at[3:4]),
        (vol.at[pl.ds(1 - core, 3)], near.at[0:3]),
        (cot.at[pl.ds(3 * (1 - core), 1)], near.at[3:4]),
        (vol, vol_out),
        (cot, cot_out),
    ]
    copies = [pltpu.make_async_copy(src, dst, sems.at[i]) for i, (src, dst) in enumerate(moves)]
    for copy in copies:
        copy.start()
    copies[0].wait()
    whole[...] = rows[...].astype(BF)
    half[...] = rows[pl.ds(13 * core, 14)].astype(BF)
    for copy in copies[1:]:
        copy.wait()


def payloads(vol, cot, master):
    vmem = pl.BlockSpec(memory_space=pltpu.VMEM)
    hbm = pl.BlockSpec(memory_space=pltpu.HBM)
    cells = pltpu.VMEM((4, SY, SZ, C), BF)
    return pl.pallas_call(
        payload_kernel,
        out_shape=(pltpu.VMEM((27, 16, C), BF), pltpu.VMEM((14, 16, C), BF)) + (cells,) * 4,
        in_specs=[hbm] * 3,
        out_specs=(vmem,) * 6,
        scratch_shapes=[pltpu.VMEM((27, 16, C), F32), pltpu.SemaphoreType.DMA((7,))],
        compiler_params=pltpu.CompilerParams(vmem_limit_bytes=8 * 2**20),
        name="payloads",
    )(*(pltpu.with_memory_space_constraint(a, pltpu.HBM) for a in (vol, cot, master.reshape(27, 64, C))))


SIDE = 26 * SZ // 16


def relay_kernel(stack, vol, cot, far, even, odd):
    gx, gy, core, dp, quarter = position()
    parity = lax.rem(gy, 2)
    for out, upper in ((even, 1 - parity), (odd, parity)):
        three, one = pl.ds(upper * (SY - 3), 3), pl.ds(upper * (SY - 1), 1)
        groups = [vol[:, three], far[0:3, three], cot[:, one], far[3:4, one]]
        out[0:41] = stack[...]
        out[41 : 41 + SIDE] = jnp.concatenate([g.reshape(-1, SZ, C) for g in groups]).reshape(SIDE, 16, C)


def relay(stack, vol, cot, far):
    vmem = pl.BlockSpec(memory_space=pltpu.VMEM)
    both = jax.ShapeDtypeStruct((41 + SIDE, 16, C), BF)
    return pl.pallas_call(
        relay_kernel,
        out_shape=(both, both),
        in_specs=[vmem] * 4,
        out_specs=(vmem,) * 2,
        compiler_params=pltpu.CompilerParams(vmem_limit_bytes=8 * 2**20),
        name="relay",
    )(stack, vol, cot, far)


def prepare_kernel(vol, cot, near, far, even, odd, mate_even, mate_odd, field, upstream):
    gx, gy, core, dp, quarter = position()
    parity = lax.rem(gy, 2)

    def ordered(first, second, swap):
        return jnp.where(swap == 0, first, second), jnp.where(swap == 0, second, first)

    def side_of(ref):
        return ref[41 : 41 + SIDE].reshape(26, SZ, C).astype(F32)

    left, right = ordered(far[...].astype(F32), near[...].astype(F32), core)
    sides = []
    lower, upper = ordered(side_of(odd), side_of(even), parity)
    mate_lower, mate_upper = ordered(side_of(mate_odd), side_of(mate_even), parity)
    for side, mate, outside in ((lower, mate_lower, gy == 0), (upper, mate_upper, gy == 3)):
        mate_planes = jnp.where(core == 0, mate[0:9], mate[3:12])
        mate_plane = jnp.where(core == 0, mate[21:22], mate[24:25])
        first, last = ordered(side[12:21], mate_planes, core)
        planes = jnp.concatenate([first, side[0:12], last]).reshape(10, 3, SZ, C)
        sides.append(jnp.where(outside, 0.0, planes))
        first, last = ordered(side[25:26], mate_plane, core)
        planes = jnp.concatenate([first, side[21:25], last]).reshape(6, 1, SZ, C)
        sides.append(jnp.where(outside, 0.0, planes))
    own = jnp.concatenate([left[0:3], vol[...].astype(F32), right[0:3]], axis=0)
    store_triple(field, slice(0, 1760), jnp.concatenate([sides[0], own, sides[2]], axis=1))
    own = jnp.concatenate([left[3:4], cot[...].astype(F32), right[3:4]], axis=0)
    upstream[...] = jnp.concatenate([sides[1], own, sides[3]], axis=1)


def prepare(vol, cot, near, far, even, odd, mate_even, mate_odd):
    vmem = pl.BlockSpec(memory_space=pltpu.VMEM)
    return pl.pallas_call(
        prepare_kernel,
        out_shape=(
            jax.ShapeDtypeStruct((10 * 176, 3 * C), BF),
            jax.ShapeDtypeStruct((6, 18, SZ, C), F32),
        ),
        in_specs=[vmem] * 8,
        out_specs=(vmem, vmem),
        compiler_params=pltpu.CompilerParams(vmem_limit_bytes=16 * 2**20),
        cost_estimate=pl.CostEstimate(flops=4_000_000, bytes_accessed=3_000_000, transcendentals=0),
        name="prepare",
    )(vol, cot, near, far, even, odd, mate_even, mate_odd)


def halves(grads, core, keep, send):
    for shard in range(2):
        keep[shard] = grads[pl.ds(13 * shard + 7 * core, 7)].reshape(16, PIECE, C)
        send[shard] = grads[pl.ds(13 * shard + 7 * (1 - core), 7)].reshape(16, PIECE, C).astype(send.dtype)


def forward_kernel(field, upstream, master, *rest):
    pieces = rest[:8]
    act, dlt, slope, flipped, send, keep = rest[8:14]
    taps, hid, grads = rest[14:]
    gx, gy, core, dp, quarter = position()

    taps[pl.ds(dp * 27, 27)] = master[...].astype(BF).reshape(27, 64, C)
    for index, piece in enumerate(pieces):
        owner_core = core if index < 4 else 1 - core
        rows = pl.ds(pl.multiple_of((quarter ^ (0, 1, 3, 2)[index % 4]) * 16, 16), 16)
        whole = dp ^ (1 + owner_core)
        taps[pl.ds(whole * 27, 27), rows, :] = piece[0:27]
        taps[pl.ds((dp ^ 3) * 27 + 13 * owner_core, 14), rows, :] = piece[27:41]
    tap_rows = taps[...].reshape(54 * C, C)

    weights = layer_weights(tap_rows, 0)
    slopes = []
    for at in range(0, 8, PLANES_ONE):
        first = conv_planes(field, at, PLANES_ONE, 22, weights)
        x_at = lax.broadcasted_iota(jnp.int32, first.shape, 0) + (gx * SX - 2 + at)
        y_at = lax.broadcasted_iota(jnp.int32, first.shape, 1) + (gy * SY - 2)
        inside = (x_at >= 0) & (x_at < NX) & (y_at >= 0) & (y_at < NY)
        store_triple(hid, slice(at * 160, (at + PLANES_ONE) * 160), jnp.where(inside, gelu_value(first), 0.0))
        begin, end = max(at, 2) - at, min(at + PLANES_ONE, 6) - at
        if begin < end:
            slopes.append(gelu_slope(first[begin:end, 2:18]))
    slope[...] = jnp.concatenate(slopes)

    weights = layer_weights(tap_rows, 1)
    deltas = []
    for at in range(0, 6, PLANES_TWO):
        second = conv_planes(hid, at, PLANES_TWO, 20, weights)
        delta = upstream[at : at + PLANES_TWO] * gelu_slope(second)
        store_triple(dlt, slice(at * 144, (at + PLANES_TWO) * 144), delta)
        begin, end = max(at, 1) - at, min(at + PLANES_TWO, 5) - at
        if begin < end:
            act[at + begin - 1 : at + end - 1] = gelu_value(second[begin:end, 1:17]).astype(BF)
            deltas.append(delta[begin:end, 1:17])
    grad_taps(grads, hid, 20, 1, 1, jnp.concatenate(deltas))
    halves(grads, core, keep, send)

    for t in range(27):
        a, b, c = t // 9, t // 3 % 3, t % 3
        row = (27 + 26 - t) * C
        block = jnp.transpose(tap_rows[row : row + C].astype(F32)).astype(BF)
        flipped[(3 * a + c) * C : (3 * a + c + 1) * C, b * C : (b + 1) * C] = block


def backward_kernel(field, dlt, slope, flipped, send, keep, grads):
    weights = flipped[...]
    back = [conv_planes(dlt, at, PLANES_BACK, 18, weights) for at in range(0, 4, PLANES_BACK)]
    grad_taps(grads, field, 22, 2, 2, jnp.concatenate(back) * slope[...])
    halves(grads, lax.axis_index("c"), keep, send)


GRADIENT = (2, 16, PIECE, C)


def forward(field, upstream, master, pieces):
    vmem = pl.BlockSpec(memory_space=pltpu.VMEM)
    return pl.pallas_call(
        forward_kernel,
        out_shape=(
            jax.ShapeDtypeStruct((SX, SY, SZ, C), BF),
            jax.ShapeDtypeStruct((6 * 144, 3 * C), BF),
            jax.ShapeDtypeStruct((SX, SY, SZ, C), F32),
            jax.ShapeDtypeStruct((9 * C, 3 * C), BF),
            jax.ShapeDtypeStruct(GRADIENT, F32),
            jax.ShapeDtypeStruct(GRADIENT, F32),
        ),
        in_specs=[vmem] * 11,
        out_specs=(vmem,) * 6,
        scratch_shapes=[
            pltpu.VMEM((108, 64, C), BF),
            pltpu.VMEM((8 * 160, 3 * C), BF),
            pltpu.VMEM((27, C, C), F32),
        ],
        compiler_params=pltpu.CompilerParams(vmem_limit_bytes=40 * 2**20),
        cost_estimate=pl.CostEstimate(flops=2_500_000_000, bytes_accessed=8_000_000, transcendentals=1_000_000),
        name="forward",
    )(field, upstream, master, *pieces)


def backward(field, dlt, slope, flipped):
    vmem = pl.BlockSpec(memory_space=pltpu.VMEM)
    return pl.pallas_call(
        backward_kernel,
        out_shape=(jax.ShapeDtypeStruct(GRADIENT, BF), jax.ShapeDtypeStruct(GRADIENT, F32)),
        in_specs=[vmem] * 4,
        out_specs=(vmem,) * 2,
        scratch_shapes=[pltpu.VMEM((27, C, C), F32)],
        compiler_params=pltpu.CompilerParams(vmem_limit_bytes=32 * 2**20),
        cost_estimate=pl.CostEstimate(flops=8_000_000_000, bytes_accessed=8_000_000, transcendentals=0),
        name="backward",
    )(field, dlt, slope, flipped)


def pair_kernel(keep_one, got_one, keep_two, got_two, out):
    for layer, (keep, got) in enumerate(((keep_one, got_one), (keep_two, got_two))):
        for shard in range(2):
            total = keep[shard] + got[shard].astype(F32)
            for piece in range(16):
                out[piece, 2 * layer + shard] = total[piece].astype(BF)


def pair_sum(keep_one, got_one, keep_two, got_two):
    vmem = pl.BlockSpec(memory_space=pltpu.VMEM)
    return pl.pallas_call(
        pair_kernel,
        out_shape=jax.ShapeDtypeStruct((16, 4, PIECE, C), BF),
        in_specs=[vmem] * 4,
        out_specs=vmem,
        compiler_params=pltpu.CompilerParams(vmem_limit_bytes=16 * 2**20),
        name="pair_sum",
    )(keep_one, got_one, keep_two, got_two)


def plane_kernel(parts, out):
    for shard in range(4):
        total = parts[0, shard].astype(F32)
        for sender in range(1, 16):
            total = total + parts[sender, shard].astype(F32)
        out[2 * shard] = total.astype(BF)
        out[2 * shard + 1] = total.astype(BF)


def plane_sum(parts):
    vmem = pl.BlockSpec(memory_space=pltpu.VMEM)
    return pl.pallas_call(
        plane_kernel,
        out_shape=jax.ShapeDtypeStruct((8, PIECE, C), BF),
        in_specs=[vmem],
        out_specs=vmem,
        compiler_params=pltpu.CompilerParams(vmem_limit_bytes=8 * 2**20),
        name="plane_sum",
    )(parts)


OWN_ROWS = HALF - C // 2
CHUNKS = 4


def adam_kernel(own_step, rows_now, *refs):
    sources, (master, one, two) = refs[: 1 if own_step else 2], refs[1 if own_step else 2 :][:3]
    new_master, new_one, new_two, grad, parts, sems = refs[-6:]
    core, odd = lax.axis_index("c"), lax.rem(lax.axis_index("dp"), 2)
    half = TAPS // 2
    owned = ((sources[0], core, range(half)),)
    if not own_step:
        owned = ((sources[1], 1 - core, range(half)), (sources[0], core, (half - 1, 0)))
    for source, owner, taps in owned:
        for tap in taps:
            block = jnp.transpose(source[tap * C : (tap + 1) * C].astype(F32))
            grad[pl.ds(pl.multiple_of((owner * half + tap) * C, C), C), :] = block
    begin = core * HALF if own_step else (1 - core) * OWN_ROWS
    size = rows_now // CHUNKS
    copies = []
    for chunk in range(CHUNKS):
        start = pl.multiple_of(begin + chunk * size, 16)
        rows, held = pl.ds(start, size), pl.ds(chunk * size, size)
        gradient = grad[pl.ds(pl.multiple_of(start + odd * (C // 2), 16), size), :]
        first = beta_one * one[rows, :] + (1.0 - beta_one) * gradient
        second = beta_two * two[rows, :] + (1.0 - beta_two) * gradient * gradient
        update = first / (1.0 - beta_one**10) / (jnp.sqrt(second / (1.0 - beta_two**10)) + epsilon)
        parts[0, held, :] = master[rows, :] - learn_rate * update
        parts[1, held, :] = first
        parts[2, held, :] = second
        for index, out in enumerate((new_master, new_one, new_two)):
            copy = pltpu.make_async_copy(parts.at[index, held], out.at[rows], sems.at[chunk, index])
            copy.start()
            copies.append(copy)
    for copy in copies:
        copy.wait()


def adam_step(own_step, sources, state, held=()):
    rows_now = OWN_ROWS if own_step else state[0].shape[0] - OWN_ROWS
    vmem = pl.BlockSpec(memory_space=pltpu.VMEM)
    hbm = pl.BlockSpec(memory_space=pl.ANY)
    inputs = len(sources) + len(state)
    return pl.pallas_call(
        functools.partial(adam_kernel, own_step, rows_now),
        out_shape=(jax.ShapeDtypeStruct(state[0].shape, F32),) * 3,
        in_specs=[vmem] * inputs + [hbm] * len(held),
        out_specs=(hbm,) * 3,
        input_output_aliases={inputs + i: i for i in range(len(held))},
        scratch_shapes=[
            pltpu.VMEM((TAPS * C, C), F32),
            pltpu.VMEM((3, rows_now, C), F32),
            pltpu.SemaphoreType.DMA((CHUNKS, 3)),
        ],
        compiler_params=pltpu.CompilerParams(vmem_limit_bytes=16 * 2**20),
        cost_estimate=pl.CostEstimate(flops=3_000_000, bytes_accessed=4_000_000, transcendentals=200_000),
        name="adam_own" if own_step else "adam_rest",
    )(*sources, *state, *held)


GX = ("zl", "x", "c")


def exchanged(cells, axis, count, by):
    return lax.ppermute(cells, axis, [(i, i ^ by) for i in range(count)])


def paired(cells, axis, count):
    pairs = [(i, i + 1) for i in range(1, count - 1, 2)]
    return lax.ppermute(cells, axis, pairs + [(j, i) for i, j in pairs])


def over_dp(whole, half):
    whole = lax.ppermute(
        whole, ("dp", "c"), [(2 * d + c, 2 * (d ^ (1 + c)) + c) for d in range(4) for c in range(2)]
    )
    return whole, exchanged(half, "dp", 4, 3)


def per_device(volume, cotangent, master, moment_one, moment_two):
    vol, cot = volume[0], cotangent[0]
    whole, half, near, far, vol, cot = payloads(vol, cot, master)
    whole, half = over_dp(whole, half)
    far = paired(far, GX, 16)
    near = exchanged(near, "c", 2, 1)

    stack = jnp.concatenate([whole, half])
    opposite = exchanged(stack, "x", 4, 1)
    even, odd = relay(stack, vol, cot, far)
    odd = exchanged(odd, "gy", 4, 3)
    even = exchanged(even, "gy", 4, 1)
    even, odd, near = lax.optimization_barrier((even, odd, near))
    mine = [stack, even, odd, opposite]
    mates = [exchanged(part, "c", 2, 1) for part in mine]
    pieces = mine + mates
    field, upstream = prepare(vol, cot, near, far, even, odd, mates[1], mates[2])
    act, dlt, slope, flipped, send_two, keep_two = forward(field, upstream, master, pieces)
    got_two = exchanged(send_two, "c", 2, 1)
    send_one, keep_one = backward(field, dlt, slope, flipped)
    got_one = exchanged(send_one, "c", 2, 1)

    spread = pair_sum(keep_one, got_one, keep_two, got_two).reshape(16, 4 * PIECE, C)
    plane = lax.all_to_all(spread, ("x", "gy"), 0, 0)
    column = lax.all_to_all(plane_sum(plane.reshape(16, 4, PIECE, C)), ("dp", "zl"), 0, 0)
    column = jnp.sum(column.astype(F32), axis=0).astype(BF)
    mine = lax.all_to_all(jnp.broadcast_to(column, (16, PIECE, C)), ("x", "gy"), 0, 0).reshape(HALF, C)
    other = exchanged(mine, "c", 2, 1)
    state = (master, moment_one, moment_two)
    held = adam_step(True, (mine,), state)
    new_master, new_one, new_two = adam_step(False, (mine, other), state, held)
    return (act[None], new_master, new_one, new_two)


def solution(mesh):
    fine = Mesh(mesh.devices.reshape(4, 2, 4, 2, 4), ("dp", "zl", "x", "c", "gy"))
    cells = P("dp", GX, "gy", None, None)
    rows = P("dp", None)
    return jax.shard_map(
        per_device,
        mesh=fine,
        in_specs=(cells, cells, rows, rows, rows),
        out_specs=(cells, rows, rows, rows),
        check_vma=False,
    )
```

```python
import functools

import jax
import jax.numpy as jnp
from jax import lax
from jax.experimental import pallas as pl
from jax.experimental.pallas import tpu as pltpu
from jax.sharding import Mesh
from jax.sharding import PartitionSpec as P

inv_root_two = 0.7071067811865476
inv_root_tau = 0.3989422804014327
beta_one = 0.9
beta_two = 0.999
learn_rate = 0.01
epsilon = 1e-08

BF = jnp.bfloat16
F32 = jnp.float32

C = 128
SX, SY, SZ = 4, 16, 8
NX, NY = 64, 64
PLANES_ONE, PLANES_TWO, PLANES_BACK = 2, 3, 2
TAPS = 14
HALF = TAPS // 2 * C
PIECE = HALF // 16


def position():
    x, core, gy = lax.axis_index("x"), lax.axis_index("c"), lax.axis_index("gy")
    gx = (lax.axis_index("zl") * 4 + x) * 2 + core
    return gx, gy, core, lax.axis_index("dp"), gy ^ (2 * lax.rem(x, 2) + lax.div(x, 2))


def gelu_value(field):
    return 0.5 * field * (1.0 + lax.erf(field * inv_root_two))


def gelu_slope(field):
    normal_cdf = 0.5 * (1.0 + lax.erf(field * inv_root_two))
    return normal_cdf + field * jnp.exp(-0.5 * field * field) * inv_root_tau


def depth_triple(field):
    depth = lax.broadcasted_iota(jnp.int32, field.shape, 2)
    below = jnp.where(depth == 0, 0.0, pltpu.roll(field, 1, 2))
    above = jnp.where(depth == SZ - 1, 0.0, pltpu.roll(field, SZ - 1, 2))
    return [part.reshape(-1, C).astype(BF) for part in (below, field, above)]


def store_triple(ref, rows, field):
    for position, part in enumerate(depth_triple(field)):
        ref[rows, position * C : (position + 1) * C] = part


def conv_planes(ref, first, planes_out, wide, weights):
    rows = planes_out * wide * SZ
    step = wide * SZ
    starts = [(first + a) * step for a in range(3)]
    left = jnp.concatenate([ref[start : start + rows, :] for start in starts], axis=1)
    prod = jnp.dot(left, weights, preferred_element_type=F32).reshape(planes_out, wide, SZ, 3 * C)
    return (
        prod[:, 0 : wide - 2, :, 0:C]
        + prod[:, 1 : wide - 1, :, C : 2 * C]
        + prod[:, 2:wide, :, 2 * C : 3 * C]
    )


def layer_weights(taps, layer):
    columns = []
    for b in range(3):
        rows = [(layer * 27 + 9 * a + 3 * b) * C for a in range(3)]
        columns.append(jnp.concatenate([taps[r : r + 3 * C] for r in rows], axis=0))
    return jnp.concatenate(columns, axis=1)


def grad_taps(grads, ref, wide, first_plane, shift, delta):
    lefts = []
    for b in range(3):
        before, after = shift + b, wide - SY - shift - b
        padded = jnp.concatenate(
            [
                jnp.zeros((SX, before, SZ, C), F32),
                delta,
                jnp.zeros((SX, after, SZ, C), F32),
            ],
            axis=1,
        ).reshape(SX * wide * SZ, C)
        lefts.append(jnp.transpose(padded).astype(BF))
    left = jnp.concatenate(lefts, axis=0)
    step = wide * SZ
    starts = [(first_plane + a) * step for a in range(3)]
    right = jnp.concatenate([ref[start : start + SX * step, :] for start in starts], axis=1)
    prod = jnp.dot(left, right, preferred_element_type=F32)
    for tap in range(27):
        a, b, c = tap // 9, tap // 3 % 3, tap % 3
        column = (3 * a + c) * C
        grads[tap] = prod[b * C : (b + 1) * C, column : column + C]


def payload_kernel(vol, cot, master, whole, half, near, far, vol_out, cot_out, rows, sems):
    gx, gy, core, dp, quarter = position()
    moves = [
        (master.at[:, pl.ds(pl.multiple_of(16 * quarter, 16), 16), :], rows),
        (vol.at[pl.ds(core, 3)], far.at[0:3]),
        (cot.at[pl.ds(3 * core, 1)], far.at[3:4]),
        (vol.at[pl.ds(1 - core, 3)], near.at[0:3]),
        (cot.at[pl.ds(3 * (1 - core), 1)], near.at[3:4]),
        (vol, vol_out),
        (cot, cot_out),
    ]
    copies = [pltpu.make_async_copy(src, dst, sems.at[i]) for i, (src, dst) in enumerate(moves)]
    for copy in copies:
        copy.start()
    copies[0].wait()
    whole[...] = rows[...].astype(BF)
    half[...] = rows[pl.ds(13 * core, 14)].astype(BF)
    for copy in copies[1:]:
        copy.wait()


def payloads(vol, cot, master):
    vmem = pl.BlockSpec(memory_space=pltpu.VMEM)
    hbm = pl.BlockSpec(memory_space=pltpu.HBM)
    cells = pltpu.VMEM((4, SY, SZ, C), BF)
    return pl.pallas_call(
        payload_kernel,
        out_shape=(pltpu.VMEM((27, 16, C), BF), pltpu.VMEM((14, 16, C), BF)) + (cells,) * 4,
        in_specs=[hbm] * 3,
        out_specs=(vmem,) * 6,
        scratch_shapes=[pltpu.VMEM((27, 16, C), F32), pltpu.SemaphoreType.DMA((7,))],
        compiler_params=pltpu.CompilerParams(vmem_limit_bytes=8 * 2**20),
        name="payloads",
    )(*(pltpu.with_memory_space_constraint(a, pltpu.HBM) for a in (vol, cot, master.reshape(27, 64, C))))


SIDE = 26 * SZ // 16


def relay_kernel(stack, vol, cot, far, even, odd):
    gx, gy, core, dp, quarter = position()
    parity = lax.rem(gy, 2)
    for out, upper in ((even, 1 - parity), (odd, parity)):
        three, one = pl.ds(upper * (SY - 3), 3), pl.ds(upper * (SY - 1), 1)
        groups = [vol[:, three], far[0:3, three], cot[:, one], far[3:4, one]]
        out[0:41] = stack[...]
        out[41 : 41 + SIDE] = jnp.concatenate([g.reshape(-1, SZ, C) for g in groups]).reshape(SIDE, 16, C)


def relay(stack, vol, cot, far):
    vmem = pl.BlockSpec(memory_space=pltpu.VMEM)
    both = jax.ShapeDtypeStruct((41 + SIDE, 16, C), BF)
    return pl.pallas_call(
        relay_kernel,
        out_shape=(both, both),
        in_specs=[vmem] * 4,
        out_specs=(vmem,) * 2,
        compiler_params=pltpu.CompilerParams(vmem_limit_bytes=8 * 2**20),
        name="relay",
    )(stack, vol, cot, far)


def prepare_kernel(vol, cot, near, far, even, odd, mate_even, mate_odd, field, upstream):
    gx, gy, core, dp, quarter = position()
    parity = lax.rem(gy, 2)

    def ordered(first, second, swap):
        return jnp.where(swap == 0, first, second), jnp.where(swap == 0, second, first)

    def side_of(ref):
        return ref[41 : 41 + SIDE].reshape(26, SZ, C).astype(F32)

    left, right = ordered(far[...].astype(F32), near[...].astype(F32), core)
    sides = []
    lower, upper = ordered(side_of(odd), side_of(even), parity)
    mate_lower, mate_upper = ordered(side_of(mate_odd), side_of(mate_even), parity)
    for side, mate, outside in ((lower, mate_lower, gy == 0), (upper, mate_upper, gy == 3)):
        mate_planes = jnp.where(core == 0, mate[0:9], mate[3:12])
        mate_plane = jnp.where(core == 0, mate[21:22], mate[24:25])
        first, last = ordered(side[12:21], mate_planes, core)
        planes = jnp.concatenate([first, side[0:12], last]).reshape(10, 3, SZ, C)
        sides.append(jnp.where(outside, 0.0, planes))
        first, last = ordered(side[25:26], mate_plane, core)
        planes = jnp.concatenate([first, side[21:25], last]).reshape(6, 1, SZ, C)
        sides.append(jnp.where(outside, 0.0, planes))
    own = jnp.concatenate([left[0:3], vol[...].astype(F32), right[0:3]], axis=0)
    store_triple(field, slice(0, 1760), jnp.concatenate([sides[0], own, sides[2]], axis=1))
    own = jnp.concatenate([left[3:4], cot[...].astype(F32), right[3:4]], axis=0)
    upstream[...] = jnp.concatenate([sides[1], own, sides[3]], axis=1)


def prepare(vol, cot, near, far, even, odd, mate_even, mate_odd):
    vmem = pl.BlockSpec(memory_space=pltpu.VMEM)
    return pl.pallas_call(
        prepare_kernel,
        out_shape=(
            jax.ShapeDtypeStruct((10 * 176, 3 * C), BF),
            jax.ShapeDtypeStruct((6, 18, SZ, C), F32),
        ),
        in_specs=[vmem] * 8,
        out_specs=(vmem, vmem),
        compiler_params=pltpu.CompilerParams(vmem_limit_bytes=16 * 2**20),
        cost_estimate=pl.CostEstimate(flops=4_000_000, bytes_accessed=3_000_000, transcendentals=0),
        name="prepare",
    )(vol, cot, near, far, even, odd, mate_even, mate_odd)


def halves(grads, core, keep, send):
    for shard in range(2):
        keep[shard] = grads[pl.ds(13 * shard + 7 * core, 7)].reshape(16, PIECE, C)
        send[shard] = grads[pl.ds(13 * shard + 7 * (1 - core), 7)].reshape(16, PIECE, C).astype(send.dtype)


def forward_kernel(field, upstream, master, *rest):
    pieces = rest[:8]
    act, dlt, slope, flipped, send, keep = rest[8:14]
    taps, hid, grads = rest[14:]
    gx, gy, core, dp, quarter = position()

    taps[pl.ds(dp * 27, 27)] = master[...].astype(BF).reshape(27, 64, C)
    for index, piece in enumerate(pieces):
        owner_core = core if index < 4 else 1 - core
        rows = pl.ds(pl.multiple_of((quarter ^ (0, 1, 3, 2)[index % 4]) * 16, 16), 16)
        whole = dp ^ (1 + owner_core)
        taps[pl.ds(whole * 27, 27), rows, :] = piece[0:27]
        taps[pl.ds((dp ^ 3) * 27 + 13 * owner_core, 14), rows, :] = piece[27:41]
    tap_rows = taps[...].reshape(54 * C, C)

    weights = layer_weights(tap_rows, 0)
    slopes = []
    for at in range(0, 8, PLANES_ONE):
        first = conv_planes(field, at, PLANES_ONE, 22, weights)
        x_at = lax.broadcasted_iota(jnp.int32, first.shape, 0) + (gx * SX - 2 + at)
        y_at = lax.broadcasted_iota(jnp.int32, first.shape, 1) + (gy * SY - 2)
        inside = (x_at >= 0) & (x_at < NX) & (y_at >= 0) & (y_at < NY)
        store_triple(hid, slice(at * 160, (at + PLANES_ONE) * 160), jnp.where(inside, gelu_value(first), 0.0))
        begin, end = max(at, 2) - at, min(at + PLANES_ONE, 6) - at
        if begin < end:
            slopes.append(gelu_slope(first[begin:end, 2:18]))
    slope[...] = jnp.concatenate(slopes)

    weights = layer_weights(tap_rows, 1)
    deltas = []
    for at in range(0, 6, PLANES_TWO):
        second = conv_planes(hid, at, PLANES_TWO, 20, weights)
        delta = upstream[at : at + PLANES_TWO] * gelu_slope(second)
        store_triple(dlt, slice(at * 144, (at + PLANES_TWO) * 144), delta)
        begin, end = max(at, 1) - at, min(at + PLANES_TWO, 5) - at
        if begin < end:
            act[at + begin - 1 : at + end - 1] = gelu_value(second[begin:end, 1:17]).astype(BF)
            deltas.append(delta[begin:end, 1:17])
    grad_taps(grads, hid, 20, 1, 1, jnp.concatenate(deltas))
    halves(grads, core, keep, send)

    for t in range(27):
        a, b, c = t // 9, t // 3 % 3, t % 3
        row = (27 + 26 - t) * C
        block = jnp.transpose(tap_rows[row : row + C].astype(F32)).astype(BF)
        flipped[(3 * a + c) * C : (3 * a + c + 1) * C, b * C : (b + 1) * C] = block


def backward_kernel(field, dlt, slope, flipped, send, keep, grads):
    weights = flipped[...]
    back = [conv_planes(dlt, at, PLANES_BACK, 18, weights) for at in range(0, 4, PLANES_BACK)]
    grad_taps(grads, field, 22, 2, 2, jnp.concatenate(back) * slope[...])
    halves(grads, lax.axis_index("c"), keep, send)


GRADIENT = (2, 16, PIECE, C)


def forward(field, upstream, master, pieces):
    vmem = pl.BlockSpec(memory_space=pltpu.VMEM)
    return pl.pallas_call(
        forward_kernel,
        out_shape=(
            jax.ShapeDtypeStruct((SX, SY, SZ, C), BF),
            jax.ShapeDtypeStruct((6 * 144, 3 * C), BF),
            jax.ShapeDtypeStruct((SX, SY, SZ, C), F32),
            jax.ShapeDtypeStruct((9 * C, 3 * C), BF),
            jax.ShapeDtypeStruct(GRADIENT, F32),
            jax.ShapeDtypeStruct(GRADIENT, F32),
        ),
        in_specs=[vmem] * 11,
        out_specs=(vmem,) * 6,
        scratch_shapes=[
            pltpu.VMEM((108, 64, C), BF),
            pltpu.VMEM((8 * 160, 3 * C), BF),
            pltpu.VMEM((27, C, C), F32),
        ],
        compiler_params=pltpu.CompilerParams(vmem_limit_bytes=40 * 2**20),
        cost_estimate=pl.CostEstimate(flops=2_500_000_000, bytes_accessed=8_000_000, transcendentals=1_000_000),
        name="forward",
    )(field, upstream, master, *pieces)


def backward(field, dlt, slope, flipped):
    vmem = pl.BlockSpec(memory_space=pltpu.VMEM)
    return pl.pallas_call(
        backward_kernel,
        out_shape=(jax.ShapeDtypeStruct(GRADIENT, BF), jax.ShapeDtypeStruct(GRADIENT, F32)),
        in_specs=[vmem] * 4,
        out_specs=(vmem,) * 2,
        scratch_shapes=[pltpu.VMEM((27, C, C), F32)],
        compiler_params=pltpu.CompilerParams(vmem_limit_bytes=32 * 2**20),
        cost_estimate=pl.CostEstimate(flops=8_000_000_000, bytes_accessed=8_000_000, transcendentals=0),
        name="backward",
    )(field, dlt, slope, flipped)


def pair_kernel(keep_one, got_one, keep_two, got_two, out):
    for layer, (keep, got) in enumerate(((keep_one, got_one), (keep_two, got_two))):
        for shard in range(2):
            total = keep[shard] + got[shard].astype(F32)
            for piece in range(16):
                out[piece, 2 * layer + shard] = total[piece].astype(BF)


def pair_sum(keep_one, got_one, keep_two, got_two):
    vmem = pl.BlockSpec(memory_space=pltpu.VMEM)
    return pl.pallas_call(
        pair_kernel,
        out_shape=jax.ShapeDtypeStruct((16, 4, PIECE, C), BF),
        in_specs=[vmem] * 4,
        out_specs=vmem,
        compiler_params=pltpu.CompilerParams(vmem_limit_bytes=16 * 2**20),
        name="pair_sum",
    )(keep_one, got_one, keep_two, got_two)


def plane_kernel(parts, out):
    for shard in range(4):
        total = parts[0, shard].astype(F32)
        for sender in range(1, 16):
            total = total + parts[sender, shard].astype(F32)
        out[2 * shard] = total.astype(BF)
        out[2 * shard + 1] = total.astype(BF)


def plane_sum(parts):
    vmem = pl.BlockSpec(memory_space=pltpu.VMEM)
    return pl.pallas_call(
        plane_kernel,
        out_shape=jax.ShapeDtypeStruct((8, PIECE, C), BF),
        in_specs=[vmem],
        out_specs=vmem,
        compiler_params=pltpu.CompilerParams(vmem_limit_bytes=8 * 2**20),
        name="plane_sum",
    )(parts)


OWN_ROWS = HALF - C // 2
CHUNKS = 4


def adam_kernel(own_step, rows_now, *refs):
    sources, (master, one, two) = refs[: 1 if own_step else 2], refs[1 if own_step else 2 :][:3]
    new_master, new_one, new_two, grad, parts, sems = refs[-6:]
    core, odd = lax.axis_index("c"), lax.rem(lax.axis_index("dp"), 2)
    half = TAPS // 2
    owned = ((sources[0], core, range(half)),)
    if not own_step:
        owned = ((sources[1], 1 - core, range(half)), (sources[0], core, (half - 1, 0)))
    for source, owner, taps in owned:
        for tap in taps:
            block = jnp.transpose(source[tap * C : (tap + 1) * C].astype(F32))
            grad[pl.ds(pl.multiple_of((owner * half + tap) * C, C), C), :] = block
    begin = core * HALF if own_step else (1 - core) * OWN_ROWS
    size = rows_now // CHUNKS
    copies = []
    for chunk in range(CHUNKS):
        start = pl.multiple_of(begin + chunk * size, 16)
        rows, held = pl.ds(start, size), pl.ds(chunk * size, size)
        gradient = grad[pl.ds(pl.multiple_of(start + odd * (C // 2), 16), size), :]
        first = beta_one * one[rows, :] + (1.0 - beta_one) * gradient
        second = beta_two * two[rows, :] + (1.0 - beta_two) * gradient * gradient
        update = first / (1.0 - beta_one**10) / (jnp.sqrt(second / (1.0 - beta_two**10)) + epsilon)
        parts[0, held, :] = master[rows, :] - learn_rate * update
        parts[1, held, :] = first
        parts[2, held, :] = second
        for index, out in enumerate((new_master, new_one, new_two)):
            copy = pltpu.make_async_copy(parts.at[index, held], out.at[rows], sems.at[chunk, index])
            copy.start()
            copies.append(copy)
    for copy in copies:
        copy.wait()


def adam_step(own_step, sources, state, held=()):
    rows_now = OWN_ROWS if own_step else state[0].shape[0] - OWN_ROWS
    vmem = pl.BlockSpec(memory_space=pltpu.VMEM)
    hbm = pl.BlockSpec(memory_space=pl.ANY)
    inputs = len(sources) + len(state)
    return pl.pallas_call(
        functools.partial(adam_kernel, own_step, rows_now),
        out_shape=(jax.ShapeDtypeStruct(state[0].shape, F32),) * 3,
        in_specs=[vmem] * inputs + [hbm] * len(held),
        out_specs=(hbm,) * 3,
        input_output_aliases={inputs + i: i for i in range(len(held))},
        scratch_shapes=[
            pltpu.VMEM((TAPS * C, C), F32),
            pltpu.VMEM((3, rows_now, C), F32),
            pltpu.SemaphoreType.DMA((CHUNKS, 3)),
        ],
        compiler_params=pltpu.CompilerParams(vmem_limit_bytes=16 * 2**20),
        cost_estimate=pl.CostEstimate(flops=3_000_000, bytes_accessed=4_000_000, transcendentals=200_000),
        name="adam_own" if own_step else "adam_rest",
    )(*sources, *state, *held)


GX = ("zl", "x", "c")


def exchanged(cells, axis, count, by):
    return lax.ppermute(cells, axis, [(i, i ^ by) for i in range(count)])


def paired(cells, axis, count):
    pairs = [(i, i + 1) for i in range(1, count - 1, 2)]
    return lax.ppermute(cells, axis, pairs + [(j, i) for i, j in pairs])


def over_dp(whole, half):
    whole = lax.ppermute(
        whole, ("dp", "c"), [(2 * d + c, 2 * (d ^ (1 + c)) + c) for d in range(4) for c in range(2)]
    )
    return whole, exchanged(half, "dp", 4, 3)


QUAD = ((0, 0), (1, 0), (0, 1), (1, 1))


def quad(part, by):
    return [
        lax.ppermute(
            part,
            ("x", "gy"),
            [(4 * i + j, 4 * (i ^ (by * ex)) + (j ^ (by * ey))) for i in range(4) for j in range(4)],
        )
        for ex, ey in QUAD[1:]
    ]


def order_kernel(*refs):
    x, gy = lax.axis_index("x"), lax.axis_index("gy")
    for ref, (fx, fy) in zip(refs[:4], QUAD):
        for slot, (ex, ey) in enumerate(QUAD):
            refs[4][4 * (x ^ (3 * fx) ^ ex) + (gy ^ (3 * fy) ^ ey)] = ref[slot]


def ordered_pieces(parts):
    vmem = pl.BlockSpec(memory_space=pltpu.VMEM)
    return pl.pallas_call(
        order_kernel,
        out_shape=jax.ShapeDtypeStruct((16, PIECE, C), BF),
        in_specs=[vmem] * 4,
        out_specs=vmem,
        compiler_params=pltpu.CompilerParams(vmem_limit_bytes=8 * 2**20),
        name="ordered_pieces",
    )(*parts)


def per_device(volume, cotangent, master, moment_one, moment_two):
    vol, cot = volume[0], cotangent[0]
    whole, half, near, far, vol, cot = payloads(vol, cot, master)
    whole, half = over_dp(whole, half)
    far = paired(far, GX, 16)
    near = exchanged(near, "c", 2, 1)

    stack = jnp.concatenate([whole, half])
    opposite = exchanged(stack, "x", 4, 1)
    even, odd = relay(stack, vol, cot, far)
    odd = exchanged(odd, "gy", 4, 3)
    even = exchanged(even, "gy", 4, 1)
    even, odd, near = lax.optimization_barrier((even, odd, near))
    mine = [stack, even, odd, opposite]
    mates = [exchanged(part, "c", 2, 1) for part in mine]
    pieces = mine + mates
    field, upstream = prepare(vol, cot, near, far, even, odd, mates[1], mates[2])
    act, dlt, slope, flipped, send_two, keep_two = forward(field, upstream, master, pieces)
    got_two = exchanged(send_two, "c", 2, 1)
    send_one, keep_one = backward(field, dlt, slope, flipped)
    got_one = exchanged(send_one, "c", 2, 1)

    spread = pair_sum(keep_one, got_one, keep_two, got_two).reshape(16, 4 * PIECE, C)
    plane = lax.all_to_all(spread, ("x", "gy"), 0, 0)
    column = lax.all_to_all(plane_sum(plane.reshape(16, 4, PIECE, C)), ("dp", "zl"), 0, 0)
    column = jnp.sum(column.astype(F32), axis=0).astype(BF)
    one = jnp.stack([column] + quad(column, 1))
    mine = ordered_pieces([one] + quad(one, 3)).reshape(HALF, C)
    other = exchanged(mine, "c", 2, 1)
    state = (master, moment_one, moment_two)
    held = adam_step(True, (mine,), state)
    new_master, new_one, new_two = adam_step(False, (mine, other), state, held)
    return (act[None], new_master, new_one, new_two)


def solution(mesh):
    fine = Mesh(mesh.devices.reshape(4, 2, 4, 2, 4), ("dp", "zl", "x", "c", "gy"))
    cells = P("dp", GX, "gy", None, None)
    rows = P("dp", None)
    return jax.shard_map(
        per_device,
        mesh=fine,
        in_specs=(cells, cells, rows, rows, rows),
        out_specs=(cells, rows, rows, rows),
        check_vma=False,
    )
```
